32 devices in a mesh: dp: 2 (over core), context: 4 (over y, x), tensor: 4 (over z).
Axes of the slice: x: 2, y: 2, z: 4, core: 2. Of those that a mesh axis runs over, the one named last changes fastest.
Arguments:
- hidden_input: bfloat16 [2, 2, 1024, 2048], P(None, 'dp', ('context', 'tensor')), may hold values from -27 to 27
- cotangent: bfloat16 [2, 2, 1024, 2048], P(None, 'dp', ('context', 'tensor')), may hold values from -6 to 6
- window_before: bfloat16 [2048], P(('dp', 'context', 'tensor')), may hold values from 0.5 to 1.5
- window_query: bfloat16 [2048, 2048], P(('dp', 'context'), 'tensor'), may hold values from -0.125 to 0.125
- window_keys: bfloat16 [2048, 256], P(('dp', 'context', 'tensor')), may hold values from -0.125 to 0.125
- window_values: bfloat16 [2048, 256], P(('dp', 'context', 'tensor')), may hold values from -0.125 to 0.125
- window_output: bfloat16 [2048, 2048], P(('dp', 'context'), 'tensor'), may hold values from -1.5 to 1.5
- window_middle: bfloat16 [2048], P(('dp', 'context', 'tensor')), may hold values from 0.5 to 1.5
- window_gate: bfloat16 [2048, 5632], P(('dp', 'context'), 'tensor'), may hold values from -0.125 to 0.125
- window_up: bfloat16 [2048, 5632], P(('dp', 'context'), 'tensor'), may hold values from -0.125 to 0.125
- window_down: bfloat16 [2048, 5632], P(('dp', 'context'), 'tensor'), may hold values from -0.078125 to 0.078125
- causal_before: bfloat16 [2048], P(('dp', 'context', 'tensor')), may hold values from 0.5 to 1.5
- causal_query: bfloat16 [2048, 2048], P(('dp', 'context'), 'tensor'), may hold values from -0.125 to 0.125
- causal_keys: bfloat16 [2048, 256], P(('dp', 'context', 'tensor')), may hold values from -0.125 to 0.125
- causal_values: bfloat16 [2048, 256], P(('dp', 'context', 'tensor')), may hold values from -0.125 to 0.125
- causal_output: bfloat16 [2048, 2048], P(('dp', 'context'), 'tensor'), may hold values from -1.5 to 1.5
- causal_middle: bfloat16 [2048], P(('dp', 'context', 'tensor')), may hold values from 0.5 to 1.5
- causal_gate: bfloat16 [2048, 5632], P(('dp', 'context'), 'tensor'), may hold values from -0.125 to 0.125
- causal_up: bfloat16 [2048, 5632], P(('dp', 'context'), 'tensor'), may hold values from -0.125 to 0.125
- causal_down: bfloat16 [2048, 5632], P(('dp', 'context'), 'tensor'), may hold values from -0.078125 to 0.078125
Outputs:
- hidden_output: bfloat16 [2, 2, 1024, 2048], P(None, 'dp', ('context', 'tensor'))
- input_grad: float32 [2, 2, 1024, 2048], P(None, 'dp', ('context', 'tensor'))
- grad_window_before: float32 [2048], P(('dp', 'context', 'tensor'))
- grad_window_query: float32 [2048, 2048], P(('dp', 'context'), 'tensor')
- grad_window_keys: float32 [2048, 256], P(('dp', 'context', 'tensor'))
- grad_window_values: float32 [2048, 256], P(('dp', 'context', 'tensor'))
- grad_window_output: float32 [2048, 2048], P(('dp', 'context'), 'tensor')
- grad_window_middle: float32 [2048], P(('dp', 'context', 'tensor'))
- grad_window_gate: float32 [2048, 5632], P(('dp', 'context'), 'tensor')
- grad_window_up: float32 [2048, 5632], P(('dp', 'context'), 'tensor')
- grad_window_down: float32 [2048, 5632], P(('dp', 'context'), 'tensor')
- grad_causal_before: float32 [2048], P(('dp', 'context', 'tensor'))
- grad_causal_query: float32 [2048, 2048], P(('dp', 'context'), 'tensor')
- grad_causal_keys: float32 [2048, 256], P(('dp', 'context', 'tensor'))
- grad_causal_values: float32 [2048, 256], P(('dp', 'context', 'tensor'))
- grad_causal_output: float32 [2048, 2048], P(('dp', 'context'), 'tensor')
- grad_causal_middle: float32 [2048], P(('dp', 'context', 'tensor'))
- grad_causal_gate: float32 [2048, 5632], P(('dp', 'context'), 'tensor')
- grad_causal_up: float32 [2048, 5632], P(('dp', 'context'), 'tensor')
- grad_causal_down: float32 [2048, 5632], P(('dp', 'context'), 'tensor')
The draws below stay inside these ranges and needn't reach their ends.
All inputs are finite; a program needn't handle non-finite values.
Results may differ from the reference program's by a relative error of at most 0.033.
Values may be sent and summed in bfloat16 or wider, within the bound.
No kernel may reach another device: no remote copies, remote signals or barrier semaphores. Data moves between devices by JAX's collectives and lax.ppermute only.
A program may use at most 320 MiB of HBM per device.

```python
import jax
import jax.numpy as jnp
from jax import lax

D = 2048
H = 32
KV = 4
HD = 64
FF = 5632
WINDOW = 512
MB = 2
SEQ = 1024
SEQS = 2


def draw_hidden_input(key, part):
    key = jax.random.fold_in(key, 11)
    base_key, row_key, column_key = jax.random.split(key, 3)
    shape = (MB, SEQS, SEQ, D)
    base = jax.random.truncated_normal(base_key, -4.0, 4.0, shape, jnp.float32)
    rows = jnp.exp(jax.random.uniform(row_key, (MB, SEQS, SEQ, 1), jnp.float32, -1.2, 1.2))
    columns = jnp.exp(jax.random.uniform(column_key, (D,), jnp.float32, -0.7, 0.7))
    return (base * rows * columns).astype(jnp.bfloat16)


def block_levels(own_key, extent, cuts, smallest, high):
    factor_of, own = 1.0, jax.random.fold_in(own_key, 6)
    for dim, blocks in cuts:
        draws = jnp.exp(jax.random.uniform(jax.random.fold_in(own, dim), (blocks,), jnp.float32, smallest / len(cuts), high / len(cuts)))
        factor_of = factor_of * jnp.repeat(draws, extent[dim] // blocks).reshape([-1 if axis == dim else 1 for axis in range(len(extent))])
    return factor_of


def normal_values(stream_key, dims, scale, bound, cuts=(), kind=jnp.bfloat16):
    array = jax.random.normal(stream_key, dims, jnp.float32) * scale
    if len(cuts) > 0:
        array = block_levels(stream_key, dims, cuts, -0.22, 0.18) * array
    return jnp.clip(array, min=-bound, max=bound).astype(kind)


def setup_inputs(seed: int = 0) -> dict:
    seeds = jax.random.split(jax.random.key(seed), 21)
    return {
        "hidden_input": draw_hidden_input(jax.random.fold_in(seeds[20], 71), 0),
        "cotangent": normal_values(seeds[1], (MB, SEQS, SEQ, D), 1.0, 6.0, ((1, 2), (2, 16))),
        "window_before": jnp.clip(1.0 + 0.1 * jax.random.normal(seeds[2], (D,), jnp.float32), 0.5, 1.5).astype(jnp.bfloat16),
        "window_query": normal_values(seeds[3], (D, H * HD), D ** -0.5, 0.125, ((0, 8), (1, 4))),
        "window_keys": normal_values(seeds[4], (D, KV * HD), D ** -0.5, 0.125, ((0, 32),)),
        "window_values": normal_values(seeds[5], (D, KV * HD), D ** -0.5, 0.125, ((0, 32),)),
        "window_output": normal_values(seeds[6], (D, H * HD), (max(1, H * HD // 128)) ** -0.5, 1.5, ((0, 8), (1, 4))),
        "window_middle": jnp.clip(1.0 + 0.1 * jax.random.normal(seeds[7], (D,), jnp.float32), 0.5, 1.5).astype(jnp.bfloat16),
        "window_gate": normal_values(seeds[8], (D, FF), D ** -0.5, 0.125, ((0, 8), (1, 4))),
        "window_up": normal_values(seeds[9], (D, FF), D ** -0.5, 0.125, ((0, 8), (1, 4))),
        "window_down": normal_values(seeds[10], (D, FF), FF ** -0.5, 0.078125, ((0, 8), (1, 4))),
        "causal_before": jnp.clip(1.0 + 0.1 * jax.random.normal(seeds[11], (D,), jnp.float32), 0.5, 1.5).astype(jnp.bfloat16),
        "causal_query": normal_values(seeds[12], (D, H * HD), D ** -0.5, 0.125, ((0, 8), (1, 4))),
        "causal_keys": normal_values(seeds[13], (D, KV * HD), D ** -0.5, 0.125, ((0, 32),)),
        "causal_values": normal_values(seeds[14], (D, KV * HD), D ** -0.5, 0.125, ((0, 32),)),
        "causal_output": normal_values(seeds[15], (D, H * HD), (max(1, H * HD // 128)) ** -0.5, 1.5, ((0, 8), (1, 4))),
        "causal_middle": jnp.clip(1.0 + 0.1 * jax.random.normal(seeds[16], (D,), jnp.float32), 0.5, 1.5).astype(jnp.bfloat16),
        "causal_gate": normal_values(seeds[17], (D, FF), D ** -0.5, 0.125, ((0, 8), (1, 4))),
        "causal_up": normal_values(seeds[18], (D, FF), D ** -0.5, 0.125, ((0, 8), (1, 4))),
        "causal_down": normal_values(seeds[19], (D, FF), FF ** -0.5, 0.078125, ((0, 8), (1, 4))),
    }


EPSILON = 1e-05
THETA = 10000.0
NEGATIVE = -1e+30

@jax.custom_vjp
def low(v):
    return lax.optimization_barrier(v.astype(jnp.bfloat16)).astype(jnp.float32)

@jax.custom_vjp
def low_back(v):
    return v

def low_keep(v):
    return (low(v), None)

def low_pass(kept, grad):
    return (grad,)

def back_keep(v):
    return (v, None)

def back_low(kept, grad):
    return (low(grad),)
low.defvjp(low_keep, low_pass)
low_back.defvjp(back_keep, back_low)

def matmul(left, right):
    return jnp.dot(left, right, precision=lax.Precision.HIGHEST, preferred_element_type=jnp.float32)

def rotate(values, positions, sign):
    half = values.shape[-1] // 2
    freq = THETA ** (-2.0 * jnp.arange(half, dtype=jnp.float32) / values.shape[-1])
    angle = positions.astype(jnp.float32)[:, None] * freq[None, :]
    cosine = jnp.cos(angle)[:, None, :]
    sine = sign * jnp.sin(angle)[:, None, :]
    first, second = (values[..., :half], values[..., half:])
    return jnp.concatenate([first * cosine - second * sine, second * cosine + first * sine], axis=-1)

def normalize(values, gain_vector):
    scale = lax.rsqrt(lax.optimization_barrier(jnp.mean(values * values, axis=-1, keepdims=True)) + EPSILON)
    return values * scale * gain_vector

def attend(query_rot, key_rot, value_low, window_len):
    group = H // KV
    keys_all = jnp.repeat(key_rot, group, axis=1)
    values_all = jnp.repeat(value_low, group, axis=1)
    rows_block = min(512, SEQ)
    key_pos = jnp.arange(SEQ, dtype=jnp.int32)

    def one_block(inputs):
        rows, start = inputs
        raw = jnp.einsum('qhd,khd->hqk', rows, keys_all, precision=lax.Precision.HIGHEST) * HD ** (-0.5)
        raw = low_back(raw)
        query_pos = start + jnp.arange(rows_block, dtype=jnp.int32)
        valid = key_pos[None, :] <= query_pos[:, None]
        if window_len > 0:
            valid = valid & (query_pos[:, None] - key_pos[None, :] < window_len)
        raw = jnp.where(valid[None], raw, NEGATIVE)
        row_max = lax.optimization_barrier(jnp.max(raw, axis=-1, keepdims=True))
        expo = jnp.exp(raw - row_max)
        probs = expo / lax.optimization_barrier(jnp.sum(expo, axis=-1, keepdims=True))
        return jnp.einsum('hqk,khd->qhd', low(probs), values_all, precision=lax.Precision.HIGHEST)
    starts = jnp.arange(SEQ // rows_block, dtype=jnp.int32) * rows_block
    mixed = lax.map(jax.checkpoint(one_block), (query_rot.reshape(SEQ // rows_block, rows_block, H, HD), starts))
    return mixed.reshape(SEQ, H, HD)

def layer(stream, params, window_len):
    before, query_w, keys_w, values_w, output_w, middle, gate_w, up_w, down_w = params
    positions = jnp.arange(SEQ, dtype=jnp.int32)
    first_in = low(normalize(stream, before))
    query_pre = low_back(matmul(first_in, query_w)).reshape(SEQ, H, HD)
    query_rot = low(rotate(query_pre, positions, 1.0))
    key_rot = low(rotate(matmul(first_in, keys_w).reshape(SEQ, KV, HD), positions, 1.0))
    value_low = low(matmul(first_in, values_w).reshape(SEQ, KV, HD))
    mixed = low(low_back(attend(query_rot, key_rot, value_low, window_len))).reshape(SEQ, H * HD)
    middle_state = stream + low_back(matmul(mixed, output_w.T))
    second_in = low(normalize(middle_state, middle))
    gate = low_back(matmul(second_in, gate_w))
    up_proj = low_back(matmul(second_in, up_w))
    hidden = low(jax.nn.silu(gate) * up_proj)
    return middle_state + low_back(matmul(hidden, down_w.T))

def reference(hidden_input, cotangent, window_before, window_query, window_keys, window_values, window_output, window_middle, window_gate, window_up, window_down, causal_before, causal_query, causal_keys, causal_values, causal_output, causal_middle, causal_gate, causal_up, causal_down):
    first_params = tuple((w.astype(jnp.float32) for w in (window_before, window_query, window_keys, window_values, window_output, window_middle, window_gate, window_up, window_down)))
    second_params = tuple((w.astype(jnp.float32) for w in (causal_before, causal_query, causal_keys, causal_values, causal_output, causal_middle, causal_gate, causal_up, causal_down)))
    inputs = hidden_input.reshape(-1, SEQ, D).astype(jnp.float32)
    cotangents = cotangent.reshape(-1, SEQ, D).astype(jnp.float32)

    def forward(stream, params_one, params_two):
        return layer(layer(stream, params_one, WINDOW), params_two, 0)

    def one_sequence(totals, pieces):
        sequence_in, sequence_cot = pieces
        result, pull = jax.vjp(forward, sequence_in, first_params, second_params)
        grad_in, grad_one, grad_two = pull(sequence_cot)
        totals = jax.tree.map(jnp.add, totals, (grad_one, grad_two))
        return (totals, (result.astype(jnp.bfloat16), grad_in))
    zeros = jax.tree.map(jnp.zeros_like, (first_params, second_params))
    totals, (outputs, in_grads) = lax.scan(one_sequence, zeros, (inputs, cotangents))
    grad_one, grad_two = totals
    return (outputs.reshape(hidden_input.shape), in_grads.reshape(hidden_input.shape), grad_one[0], grad_one[1], grad_one[2], grad_one[3], grad_one[4], grad_one[5], grad_one[6], grad_one[7], grad_one[8], grad_two[0], grad_two[1], grad_two[2], grad_two[3], grad_two[4], grad_two[5], grad_two[6], grad_two[7], grad_two[8])
```

```python
import jax
import jax.numpy as jnp
from jax import lax
from jax.sharding import PartitionSpec as P

H = 32
KV = 4
HD = 64
WINDOW = 512
EPSILON = 1e-05
THETA = 10000.0
NEGATIVE = -1e30
BF = jnp.bfloat16
F32 = jnp.float32


def swap(value, axis, bits):
    count = lax.axis_size(axis)
    return lax.ppermute(value, axis, [(source, source ^ bits) for source in range(count)])


def row_index():
    return lax.axis_index("dp") * lax.axis_size("context") + lax.axis_index("context")


def relative(values):
    index = row_index()
    count = lax.axis_size("dp") * lax.axis_size("context")
    block = values.shape[-1] // count
    lead = values.shape[:-1]
    bit = 1
    while bit < count:
        paired = values.reshape(*lead, count // (2 * bit), 2, bit * block)
        other = jnp.flip(paired, axis=-2).reshape(values.shape)
        values = jnp.where((index & bit) != 0, other, values)
        bit *= 2
    return values


def gather_rows(piece):
    count = lax.axis_size("context")
    if count != 4:
        parts, bit = [piece], 1
        while bit < count:
            parts = parts + [swap(part, "context", bit) for part in parts]
            bit *= 2
        return jnp.concatenate(parts + [swap(part, "dp", 1) for part in parts], axis=0)
    half = piece.shape[0] // 2
    by_x = swap(piece, "context", 1)
    by_y = swap(piece, "context", 2)
    far_low = swap(by_y[:half], "context", 1)
    far_high = swap(by_x[half:], "context", 2)
    parts = [piece, by_x, by_y, far_low, far_high]
    others = [swap(part, "dp", 1) for part in parts]
    return jnp.concatenate(parts + others, axis=0)


def scatter_rows(keep, send):
    both = keep.astype(F32) + swap(send, "dp", 1).astype(F32)
    count = lax.axis_size("context")
    if count != 4:
        bit = count // 2
        while bit:
            middle = both.shape[0] // 2
            both = both[:middle] + swap(both[middle:].astype(BF), "context", bit).astype(F32)
            bit //= 2
        return both
    quarter = both.shape[0] // 4
    half = quarter // 2
    blocks = [both[i * quarter : (i + 1) * quarter] for i in range(4)]
    low = [block[:half] for block in blocks]
    high = [block[half:] for block in blocks]
    low_send = jnp.concatenate([low[1], low[3]], axis=0).astype(BF)
    high_send = jnp.concatenate([high[2], high[3]], axis=0).astype(BF)
    low_got = swap(low_send, "context", 1).astype(F32)
    high_got = swap(high_send, "context", 2).astype(F32)
    low_own = low[0] + low_got[:half]
    low_next = (low[2] + low_got[half:]).astype(BF)
    high_own = high[0] + high_got[:half]
    high_next = (high[1] + high_got[half:]).astype(BF)
    low_own = low_own + swap(low_next, "context", 2).astype(F32)
    high_own = high_own + swap(high_next, "context", 1).astype(F32)
    return jnp.concatenate([low_own, high_own], axis=0)


def gather_tokens(piece):
    return lax.all_gather(piece, "tensor", axis=0, tiled=True)


def scatter_tokens(term):
    count = lax.axis_size("tensor")
    me = lax.axis_index("tensor")
    rows = term.shape[0] // count
    chunks = term.astype(BF).reshape(count, rows, term.shape[1])
    pick = lambda k: lax.dynamic_index_in_dim(chunks, me ^ k, 0, keepdims=False)
    total = pick(0).astype(F32)
    for k in range(1, count):
        total = total + swap(pick(k), "tensor", k).astype(F32)
    return total


def gather_blocks(pair):
    parts = [pair] + [swap(pair, "context", r) for r in range(1, lax.axis_size("context"))]
    return jnp.concatenate(parts, axis=0)


def scatter_blocks(both):
    count = lax.axis_size("context")
    rows = both.shape[0] // count
    total = both[:rows]
    for r in range(1, count):
        total = total + swap(both[r * rows : (r + 1) * rows].astype(BF), "context", r).astype(F32)
    return total


def dot(left, right, left_dim, right_dim):
    return lax.dot_general(
        left, right, (((left_dim,), (right_dim,)), ((), ())), preferred_element_type=F32
    )


def rotate(values, cosine, sine):
    half = values.shape[-1] // 2
    first, second = values[..., :half], values[..., half:]
    return jnp.concatenate(
        [first * cosine - second * sine, second * cosine + first * sine], axis=-1
    )


def normalize(values, gain):
    scale = lax.rsqrt(jnp.mean(values * values, axis=-1, keepdims=True) + EPSILON)
    return (values * scale * gain).astype(BF)


def norm_back(incoming, values, gain):
    scale = lax.rsqrt(jnp.mean(values * values, axis=-1, keepdims=True) + EPSILON)
    weighted = incoming * gain
    unit = values * scale
    return scale * (weighted - unit * jnp.mean(weighted * unit, axis=-1, keepdims=True))


def project(first_in, qkv_w, cosine, sine):
    heads = (qkv_w.shape[1] - 2 * HD) // HD
    pre = dot(first_in, qkv_w, 1, 0)
    turned = rotate(
        pre[:, : (heads + 1) * HD].reshape(pre.shape[0], heads + 1, HD),
        cosine[:, None],
        sine[:, None],
    )
    query = turned[:, :heads].astype(BF)
    pair = jnp.concatenate([turned[:, heads], pre[:, (heads + 1) * HD :]], axis=1).astype(BF)
    return query, pair


def scores_of(query, keys, allowed):
    raw = jnp.einsum("qhd,kd->hqk", query, keys, preferred_element_type=F32) * HD ** (-0.5)
    return jnp.where(allowed[None], raw, NEGATIVE)


def attend(query, block, allowed):
    scores = scores_of(query, block[:, :HD], allowed)
    row_max = jnp.max(scores, axis=-1, keepdims=True)
    expo = jnp.exp(scores - row_max)
    total = jnp.sum(expo, axis=-1, keepdims=True)
    probs_low = (expo / total).astype(BF)
    mixed = jnp.einsum("hqk,kd->qhd", probs_low, block[:, HD:], preferred_element_type=F32)
    return mixed.astype(BF).reshape(query.shape[0], -1), (row_max, total)


def attend_back(grad_mixed, query, block, allowed, stats):
    row_max, total = stats
    scale = HD ** (-0.5)
    grad_mixed = grad_mixed.reshape(query.shape)
    probs = jnp.exp(scores_of(query, block[:, :HD], allowed) - row_max) / total
    probs_low = probs.astype(BF)
    grad_probs = jnp.einsum("qhd,kd->hqk", grad_mixed, block[:, HD:], preferred_element_type=F32)
    inner = jnp.sum(probs * grad_probs, axis=-1, keepdims=True)
    grad_scores = (probs * (grad_probs - inner)).astype(BF)
    key_part = jnp.einsum("hqk,qhd->kd", grad_scores, query, preferred_element_type=F32) * scale
    value_part = jnp.einsum("hqk,qhd->kd", probs_low, grad_mixed, preferred_element_type=F32)
    query_part = (
        jnp.einsum("hqk,kd->qhd", grad_scores, block[:, :HD], preferred_element_type=F32) * scale
    )
    return query_part, jnp.concatenate([key_part, value_part], axis=1)


def feed(second_in, gate_up_w):
    units = gate_up_w.shape[1] // 2
    both = dot(second_in, gate_up_w, 1, 0)
    gate, up = both[:, :units], both[:, units:]
    hidden = (jax.nn.silu(gate) * up).astype(BF)
    return hidden, both


def feed_back(grad_hidden, both):
    units = both.shape[1] // 2
    gate, up = both[:, :units], both[:, units:]
    sigma = jax.nn.sigmoid(gate)
    grad_gate = grad_hidden * up * sigma * (1.0 + gate * (1.0 - sigma))
    grad_up = grad_hidden * gate * sigma
    return jnp.concatenate([grad_gate, grad_up], axis=1).astype(BF)


def weight_grad(lefts, rights):
    left = jnp.concatenate(lefts, axis=0)
    right = jnp.concatenate(rights, axis=0)
    half = left.shape[1] // 2
    keep = dot(left[:, :half], right, 0, 0).astype(BF)
    send = dot(left[:, half:], right, 0, 0).astype(BF)
    return scatter_rows(keep, send)


def per_device(hidden_input, cotangent, *params):
    layers = (params[:9], params[9:])
    tensor_count = lax.axis_size("tensor")
    rows = hidden_input.shape[2]
    block_len = rows * tensor_count
    head_count = params[1].shape[1] // HD
    heads_of = [j * head_count // (H // KV) for j in range(tensor_count)]
    context = lax.axis_index("context")
    positions = context * block_len + jnp.arange(block_len, dtype=jnp.int32)
    key_pos = jnp.concatenate(
        [
            (context ^ r) * block_len + jnp.arange(block_len, dtype=jnp.int32)
            for r in range(lax.axis_size("context"))
        ]
    )
    causal = key_pos[None, :] <= positions[:, None]
    masks = (causal & (positions[:, None] - key_pos[None, :] < WINDOW), causal)
    freq = THETA ** (-2.0 * jnp.arange(HD // 2, dtype=F32) / HD)
    angle = positions.astype(F32)[:, None] * freq[None, :]
    cosine, sine = jnp.cos(angle), jnp.sin(angle)

    streams = range(hidden_input.shape[0])
    first_low = [relative(hidden_input[i, 0]) for i in streams]
    first_all = [gather_tokens(low) for low in first_low]

    small = []
    gains = jnp.stack([layers[0][0], layers[0][5], layers[1][0], layers[1][5]], axis=1)
    gains = jnp.pad(gains, ((0, 0), (0, 2 * HD - 4)))
    for head in heads_of:
        columns = []
        for layer in layers:
            columns += [layer[2][:, head * HD : (head + 1) * HD]]
            columns += [layer[3][:, head * HD : (head + 1) * HD]]
        small.append(jnp.concatenate(columns + [gains], axis=1))
    small = lax.all_to_all(
        jnp.concatenate(small, axis=0), "tensor", split_axis=0, concat_axis=0, tiled=True
    )
    pairs_w = (small[:, : 2 * HD], small[:, 2 * HD : 4 * HD])
    gain_rows = small[:, 4 * HD :]

    weights = []
    head_group = gather_rows(jnp.concatenate([layers[0][1], pairs_w[0], gain_rows], axis=1))
    width = head_group.shape[1]
    pick = jnp.eye(8, 2 * HD, dtype=BF)
    gain_all = dot(pick, head_group[:, width - 2 * HD :], 1, 1)
    for number, layer in enumerate(layers):
        if number == 0:
            qkv_w = head_group[:, : width - 2 * HD]
        else:
            qkv_w = gather_rows(jnp.concatenate([layer[1], pairs_w[1]], axis=1))
        weights.append(
            (
                gain_all[2 * number : 2 * number + 1],
                gain_all[2 * number + 1 : 2 * number + 2],
                qkv_w,
                gather_rows(layer[4]),
                gather_rows(jnp.concatenate([layer[6], layer[7]], axis=1)),
                gather_rows(layer[8]),
            )
        )

    saved = [[None, None] for _ in streams]
    state = [low.astype(F32) for low in first_low]
    for number in range(2):
        before, middle, qkv_w, output_w, gate_up_w, down_w = weights[number]
        for i in streams:
            stream = state[i]
            if number == 0:
                first_in = normalize(first_all[i].astype(F32), before)
            else:
                first_in = gather_tokens(normalize(stream, before))
            query, pair = project(first_in, qkv_w, cosine, sine)
            block = gather_blocks(pair)
            mixed, stats = attend(query, block, masks[number])
            middle_state = stream + scatter_tokens(dot(mixed, output_w, 1, 1))
            second_in = gather_tokens(normalize(middle_state, middle))
            hidden, both = feed(second_in, gate_up_w)
            state[i] = middle_state + scatter_tokens(dot(hidden, down_w, 1, 1))
            saved[i][number] = (
                stream, first_in, query, block, stats, mixed, middle_state, second_in, both, hidden
            )
    outputs = [relative(value.astype(BF)) for value in state]

    incoming = [relative(cotangent[i, 0]) for i in streams]
    large = [None, None]
    for number in (1, 0):
        before, middle, qkv_w, output_w, gate_up_w, down_w = weights[number]
        kept = []
        for i in streams:
            stream, first_in, query, block, stats, mixed, middle_state, second_in, both, hidden = (
                saved[i][number]
            )
            grad_low = gather_tokens(incoming[i].astype(BF))
            grad_both = feed_back(dot(grad_low, down_w, 1, 0), both)
            reduced_two = scatter_tokens(dot(grad_both, gate_up_w, 1, 1))
            grad_mid = incoming[i].astype(F32) + norm_back(reduced_two, middle_state, middle)
            mid_low = gather_tokens(grad_mid.astype(BF))
            grad_mixed = dot(mid_low, output_w, 1, 0).astype(BF)
            query_part, pair_part = attend_back(grad_mixed, query, block, masks[number], stats)
            pair_part = scatter_blocks(pair_part)
            grad_query = rotate(query_part, cosine[:, None], -sine[:, None]).reshape(block_len, -1)
            grad_key = rotate(pair_part[:, :HD], cosine, -sine)
            grad_qkv = jnp.concatenate(
                [grad_query, grad_key, pair_part[:, HD:]], axis=1
            ).astype(BF)
            reduced_one = scatter_tokens(dot(grad_qkv, qkv_w, 1, 1))
            incoming[i] = grad_mid + norm_back(reduced_one, stream, before)
            kept.append((first_in, grad_qkv, mid_low, mixed, second_in, grad_both, grad_low, hidden))
        kept = list(zip(*kept))
        large[number] = (
            weight_grad(kept[0], kept[1]),
            weight_grad(kept[2], kept[3]),
            weight_grad(kept[4], kept[5]),
            weight_grad(kept[6], kept[7]),
        )
    in_grads = [relative(value) for value in incoming]

    columns = []
    sums = []
    for number, layer in enumerate(layers):
        qkv_g, _, gate_up_g, _ = large[number]
        own_qkv = jnp.concatenate([layer[1], pairs_w[number]], axis=1).astype(F32)
        own_gate_up = jnp.concatenate([layer[6], layer[7]], axis=1).astype(F32)
        own_gains = gain_rows[:, 2 * number : 2 * number + 2].astype(F32)
        sums.append(jnp.sum(own_qkv * qkv_g, axis=1, keepdims=True) / own_gains[:, :1])
        sums.append(jnp.sum(own_gate_up * gate_up_g, axis=1, keepdims=True) / own_gains[:, 1:])
        columns.append(qkv_g[:, qkv_g.shape[1] - 2 * HD :])
    tail = jnp.pad(jnp.concatenate(sums, axis=1), ((0, 0), (0, 2 * HD - 4)))
    small_g = lax.all_to_all(
        jnp.concatenate(columns + [tail], axis=1), "tensor", split_axis=0, concat_axis=0, tiled=True
    ).reshape(tensor_count, -1, 6 * HD)
    gain_g = jnp.sum(small_g[:, :, 4 * HD : 4 * HD + 4], axis=0)

    results = [jnp.stack(outputs)[:, None], jnp.stack(in_grads)[:, None]]
    for number, layer in enumerate(layers):
        qkv_g, output_g, gate_up_g, down_g = large[number]
        units = layer[6].shape[1]
        pair_g = []
        for part in range(2):
            at = (2 * number + part) * HD
            heads = []
            for head in range(KV):
                pieces = [
                    small_g[j, :, at : at + HD] for j in range(tensor_count) if heads_of[j] == head
                ]
                heads.append(sum(pieces))
            pair_g.append(jnp.concatenate(heads, axis=1))
        results += [
            gain_g[:, 2 * number],
            qkv_g[:, : layer[1].shape[1]],
            pair_g[0],
            pair_g[1],
            output_g,
            gain_g[:, 2 * number + 1],
            gate_up_g[:, :units],
            gate_up_g[:, units:],
            down_g,
        ]
    return tuple(results)


def solution(mesh):
    rows = P(("dp", "context", "tensor"))
    tall = P(("dp", "context", "tensor"), None)
    wide = P(("dp", "context"), "tensor")
    tokens = P(None, "dp", ("context", "tensor"), None)
    layer = (rows, wide, tall, tall, wide, rows, wide, wide, wide)
    return jax.shard_map(
        per_device,
        mesh=mesh,
        in_specs=(tokens, tokens) + layer + layer,
        out_specs=(tokens, tokens) + layer + layer,
        check_vma=False,
    )
```

```python
import functools

import jax
import jax.numpy as jnp
from jax import lax
from jax.experimental import pallas as pl
from jax.experimental.pallas import tpu as pltpu
from jax.sharding import PartitionSpec as P

H = 32
KV = 4
HD = 64
WINDOW = 512
EPSILON = 1e-05
THETA = 10000.0
NEGATIVE = -1e30
BF = jnp.bfloat16
F32 = jnp.float32
PAIR = 2 * HD
COST = {
    "project": 5.0,
    "attend": 12.0,
    "attend_back": 13.0,
    "project_back": 5.0,
    "feed": 13.0,
    "feed_back": 15.0,
    "weight_grads": 11.0,
    "keep_kernel": 13.0,
    "fold": 6.0,
    "finish_ffn": 6.0,
    "stacked": 4.0,
}
WEIGHT = 3.0e6
VMEM_LIMIT = 60 * 1024 * 1024


def swap(value, axis, bits):
    count = lax.axis_size(axis)
    return lax.ppermute(value, axis, [(source, source ^ bits) for source in range(count)])


def gather_near(stack):
    if lax.axis_size("context") != 4:
        return [stack]
    return [stack, swap(stack, "context", 1), swap(stack, "context", 2)]


def gather_far(parts, queue):
    count = lax.axis_size("context")
    if count == 4:
        low, high = halves(parts[2], parts[1], queue)
        parts = parts + [swap(low, "context", 1), swap(high, "context", 2)]
    else:
        bit = 1
        while bit < count:
            parts = parts + [swap(part, "context", bit) for part in parts]
            bit *= 2
    return parts + [swap(part, "dp", 1) for part in parts]


def segments(parts, low, high, block):
    found = []
    side = len(parts) // 2
    full = parts[0].shape[0]
    for core in range(2):
        feature = core * (side - (1 if side == 5 else 0)) * block
        for number in range(side):
            at = core * side + number
            if side == 5 and number >= 3:
                cut = full // 2
                start, stop = (0, cut) if number == 3 else (cut, full)
                first, last = max(low, start), min(high, stop)
                if first < last:
                    found.append((at, first - start, last - first, feature + 3 * block + first - low))
            else:
                found.append((at, low, high - low, feature + number * block))
    return found


def gather_tokens(piece):
    return lax.all_gather(piece, "tensor", axis=0, tiled=True)


def exchange_tokens(chunks):
    return [chunks[0]] + [swap(chunks[k], "tensor", k) for k in range(1, len(chunks))]


def exchange_blocks(pieces):
    return [pieces[0]] + [swap(pieces[r], "context", r) for r in range(1, len(pieces))]


def dot(left, right, left_dim, right_dim):
    return lax.dot_general(
        left, right, (((left_dim,), (right_dim,)), ((), ())), preferred_element_type=F32
    )


class Queue:
    def __init__(self, place):
        self.place = place
        self.last = None
        self.due = []


def call(kernel, outs, ins, queue, grid=(1,), in_specs=None, out_specs=None, scratch=()):
    whole = lambda x: pl.BlockSpec(x.shape, lambda *i, n=len(x.shape): (0,) * n)
    in_specs = [whole(x) if s is None else s for x, s in zip(ins, in_specs or [None] * len(ins))]
    out_specs = [whole(x) if s is None else s for x, s in zip(outs, out_specs or [None] * len(outs))]
    before = [x for x in [queue.last] + queue.due if x is not None]
    queue.due = []
    count = len(ins)
    name = kernel.__qualname__.split(".")[0]
    if "fold" in kernel.__qualname__ or "keep" in kernel.__qualname__:
        name = kernel.__qualname__.split(".")[-1]

    def ordered(place, *refs):
        kernel(place, *refs[:count], *refs[count + len(before) :])

    found = list(pl.pallas_call(
        ordered,
        name=name,
        out_shape=outs,
        grid_spec=pltpu.PrefetchScalarGridSpec(
            num_scalar_prefetch=1,
            grid=grid,
            in_specs=in_specs + [pl.BlockSpec(memory_space=pl.ANY)] * len(before),
            out_specs=out_specs,
            scratch_shapes=list(scratch),
        ),
        compiler_params=pltpu.CompilerParams(
            vmem_limit_bytes=VMEM_LIMIT, dimension_semantics=("arbitrary",) * len(grid)
        ),
        cost_estimate=pl.CostEstimate(
            flops=int(COST.get(name, 3.0) * 1 * 1.0e9), bytes_accessed=int(COST.get(name, 3.0) * 1 * 3.0e6), transcendentals=0
        ),
    )(queue.place, *ins, *before))
    queue.last = min(found, key=lambda x: x.size)
    return found


def shape(dims, dtype=BF):
    return jax.ShapeDtypeStruct(dims, dtype)


def stacked(pieces, queue):
    rows, columns = pieces[0].shape

    def kernel(place, *refs):
        for number, source in enumerate(refs[:-1]):
            @pl.when(pl.program_id(0) == number)
            def _(source=source):
                refs[-1][...] = source[...]

    return call(
        kernel,
        [shape((len(pieces) * rows, columns))],
        pieces,
        queue,
        grid=(len(pieces),),
        out_specs=[pl.BlockSpec((rows, columns), lambda i, place: (i, 0))],
    )[0]


def halves(first, second, queue):
    rows, columns = first.shape
    half = rows // 2

    def kernel(place, first_ref, second_ref, upper, lower):
        upper[...] = first_ref[...]
        lower[...] = second_ref[...]

    return call(
        kernel,
        [shape((half, columns))] * 2,
        [first, second],
        queue,
        in_specs=[
            pl.BlockSpec((half, columns), lambda i, place: (0, 0)),
            pl.BlockSpec((half, columns), lambda i, place: (1, 0)),
        ],
    )


def placed(pieces, queue):
    rows, columns = pieces[0].shape

    def kernel(place, *refs):
        for k, source in enumerate(refs[:-1]):
            at = pl.multiple_of((place[2] ^ k) * rows, rows)
            refs[-1][pl.ds(at, rows), :] = source[...]

    return call(kernel, [shape((len(pieces) * rows, columns))], pieces, queue)[0]


def gain_vectors(kvg, kv_at, width, queue):
    def kernel(place, *refs):
        row = lax.broadcasted_iota(jnp.int32, (8, PAIR), 0)
        pick = (row == lax.broadcasted_iota(jnp.int32, (8, PAIR), 1)).astype(BF)
        for at, low, rows, feature in kv_at:
            refs[-1][:, feature : feature + rows] = dot(pick, refs[at][low : low + rows, :], 1, 1)

    return call(
        kernel,
        [shape((8, width), F32)],
        kvg,
        queue,
        in_specs=[pl.BlockSpec((p.shape[0], PAIR), lambda i, place: (0, 2)) for p in kvg],
    )[0]


def reorder(pieces, queue):
    width = pieces[0].shape[-1]
    count = 2 * lax.axis_size("context")
    block = width // count

    def kernel(place, *refs):
        for source, target in zip(refs[: len(pieces)], refs[len(pieces) :]):
            for r in range(count):
                at = pl.multiple_of((place[0] ^ r) * block, block)
                target[:, r * block : (r + 1) * block] = source[:, pl.ds(at, block)]

    return call(kernel, [shape(p.shape, p.dtype) for p in pieces], pieces, queue)


def turned(tile, cosine, sine):
    lane = lax.broadcasted_iota(jnp.int32, tile.shape, 1)
    half = HD // 2
    other = jnp.where(
        lane % HD < half, pltpu.roll(tile, PAIR - half, 1), pltpu.roll(tile, half, 1)
    )
    return tile * cosine + other * sine


def keys_only(table, fill):
    lane = lax.broadcasted_iota(jnp.int32, table.shape, 1)
    return jnp.where(lane < HD, table, fill)


def put_chunks(place, outs, total):
    rows = outs[0].shape[0]
    for k, out in enumerate(outs):
        at = pl.multiple_of((place[2] ^ k) * rows, rows)
        out[...] = total[pl.ds(at, rows), :].astype(BF)


def project(sources, gain, qo, qo_at, kvg, kv_at, tables, queue):
    piece_rows, width = sources[0].shape
    tokens = piece_rows * len(sources)
    columns = qo[0].shape[1]
    raw = gain is not None
    count = len(qo)

    def kernel(place, *refs):
        if raw:
            refs, (query, pair, normed) = refs[:-3], refs[-3:]
            gain_ref, refs = refs[0], refs[1:]
        else:
            refs, (query, pair) = refs[:-2], refs[-2:]
        source_refs, refs = refs[: len(sources)], refs[len(sources) :]
        source = source_refs[0]
        qo_refs, kv_refs, (cos_ref, sin_ref) = refs[:count], refs[count:-2], refs[-2:]
        if raw:
            for k, piece in enumerate(source_refs):
                values = piece[...].astype(F32)
                scale = lax.rsqrt(jnp.mean(values * values, axis=1, keepdims=True) + EPSILON)
                at = 0
                if len(sources) > 1:
                    at = pl.multiple_of((place[2] ^ k) * piece_rows, piece_rows)
                normed[pl.ds(at, piece_rows), :] = (values * scale * gain_ref[...]).astype(BF)
            source = normed
        cosine, sine = cos_ref[...], sin_ref[...]
        pre = 0.0
        for at, low, rows, feature in qo_at:
            pre += dot(source[:, feature : feature + rows], qo_refs[at][low : low + rows, :], 1, 0)
        for tile in range(columns // PAIR):
            part = slice(tile * PAIR, (tile + 1) * PAIR)
            query[:, part] = turned(pre[:, part], cosine, sine).astype(BF)
        pre = 0.0
        for at, low, rows, feature in kv_at:
            pre += dot(source[:, feature : feature + rows], kv_refs[at][low : low + rows, :], 1, 0)
        pair[...] = turned(pre, keys_only(cosine, 1.0), keys_only(sine, 0.0)).astype(BF)

    outs = [shape((tokens, columns)), shape((tokens, PAIR))]
    if raw:
        outs.append(shape((tokens, width)))
    ins = ([gain] if raw else []) + list(sources) + list(qo) + list(kvg[1]) + list(tables)
    layer = kvg[0]
    in_specs = [None] * (len(ins) - len(kvg[1]) - 2)
    in_specs += [
        pl.BlockSpec((part.shape[0], PAIR), lambda i, place: (0, layer)) for part in kvg[1]
    ]
    in_specs += [None, None]
    found = call(
        kernel,
        outs,
        ins,
        queue,
        in_specs=in_specs,
    )
    return found if raw else found + [sources[0]]


def mask_bias(place, bias, tokens, blocks, is_window):
    query_pos = place[1] * tokens + lax.broadcasted_iota(jnp.int32, (tokens, tokens), 1)
    key_row = lax.broadcasted_iota(jnp.int32, (tokens, tokens), 0)
    for r in range(blocks):
        key_pos = (place[1] ^ r) * tokens + key_row
        allowed = key_pos <= query_pos
        if is_window:
            allowed = allowed & (query_pos - key_pos < WINDOW)
        bias[r * tokens : (r + 1) * tokens, :] = jnp.where(allowed, 0.0, NEGATIVE)


def head_masks(tokens):
    lane = lax.broadcasted_iota(jnp.int32, (tokens, PAIR), 1)
    return (lane < HD, lane >= HD)


def attend(query, blocks, qo, o_at, is_window, width, queue):
    tokens, columns = query.shape
    heads = columns // HD
    count, many = len(blocks), len(qo)
    total_keys = count * tokens
    chunks = lax.axis_size("tensor")

    def kernel(place, query_ref, *refs):
        block_refs, refs = refs[:count], refs[count:]
        qo_refs, refs = refs[:many], refs[many:]
        mixed, stats, refs = refs[0], refs[1], refs[2:]
        outs, (bias, keys_twice, values_t, total) = refs[:chunks], refs[chunks:]
        mask_bias(place, bias, tokens, count, is_window)
        for r in range(count):
            rows = slice(r * tokens, (r + 1) * tokens)
            both = block_refs[r][...].astype(F32)
            first = keys_only(both, 0.0)
            keys_twice[rows, :] = (first + pltpu.roll(first, HD, 1)).astype(BF)
            values_t[:, rows] = pltpu.roll(both, HD, 1).T[:HD, :].astype(BF)
        masks = head_masks(tokens)

        def one_pair(number, carry):
            at = pl.multiple_of(number * PAIR, PAIR)
            queries = query_ref[:, pl.ds(at, PAIR)].astype(F32) * HD ** (-0.5)
            parts = []
            for side in range(2):
                own = jnp.where(masks[side], queries, 0.0).astype(BF)
                scores = dot(keys_twice[...], own, 1, 1) + bias[...]
                top = jnp.max(scores, axis=0, keepdims=True)
                expo = jnp.exp(scores - top)
                amount = jnp.sum(expo, axis=0, keepdims=True)
                parts.append(dot(values_t[...], expo.astype(BF), 1, 0) * (1.0 / amount))
                stats[2 * number + side] = top + jnp.log(amount)
            mixed[:, pl.ds(at, PAIR)] = jnp.concatenate(parts, axis=0).T.astype(BF)
            return carry

        lax.fori_loop(0, heads // 2, one_pair, 0)
        for at, low, rows, feature in o_at:
            total[:, feature : feature + rows] = dot(
                mixed[...], qo_refs[at][low : low + rows, :], 1, 1
            )
        put_chunks(place, outs, total)

    outs = [shape((tokens, columns)), shape((heads, 1, tokens), F32)]
    outs += [shape((tokens // chunks, width)) for _ in range(chunks)]
    found = call(
        kernel,
        outs,
        [query] + list(blocks) + list(qo),
        queue,
        scratch=[
            pltpu.VMEM((total_keys, tokens), F32),
            pltpu.VMEM((total_keys, PAIR), BF),
            pltpu.VMEM((HD, total_keys), BF),
            pltpu.VMEM((tokens, width), F32),
        ],
    )
    return found[0], found[1], found[2:]


def attend_back(mid_low, query, blocks, stats, qo, o_at, tables, is_window, queue):
    tokens, columns = query.shape
    width = mid_low.shape[1]
    heads = columns // HD
    count, many = len(blocks), len(qo)
    total_keys = count * tokens

    def kernel(place, mid_ref, query_ref, stats_ref, cos_ref, sin_ref, *refs):
        block_refs, refs = refs[:count], refs[count:]
        qo_refs, refs = refs[:many], refs[many:]
        grad_query, refs = refs[0], refs[1:]
        outs, refs = refs[:count], refs[count:]
        bias, keys_twice, values_twice, keys_t, grad_mixed, key_sum, value_sum = refs
        pre = 0.0
        for at, low, rows, feature in o_at:
            pre += dot(mid_ref[:, feature : feature + rows], qo_refs[at][low : low + rows, :], 1, 0)
        grad_mixed[...] = pre.astype(BF)
        mask_bias(place, bias, tokens, count, is_window)
        for r in range(count):
            rows = slice(r * tokens, (r + 1) * tokens)
            both = block_refs[r][...].astype(F32)
            first = keys_only(both, 0.0)
            last = both - first
            keys_twice[rows, :] = (first + pltpu.roll(first, HD, 1)).astype(BF)
            values_twice[rows, :] = (last + pltpu.roll(last, HD, 1)).astype(BF)
            keys_t[:, rows] = both.T[:HD, :].astype(BF)
        key_sum[...] = jnp.zeros_like(key_sum)
        value_sum[...] = jnp.zeros_like(value_sum)
        masks = head_masks(tokens)
        cosine, sine = cos_ref[...], sin_ref[...]

        def one_pair(number, carry):
            at = pl.multiple_of(number * PAIR, PAIR)
            queries = query_ref[:, pl.ds(at, PAIR)].astype(F32) * HD ** (-0.5)
            grads = grad_mixed[:, pl.ds(at, PAIR)].astype(F32)
            parts = []
            for side in range(2):
                own = jnp.where(masks[side], queries, 0.0).astype(BF)
                grad_own = jnp.where(masks[side], grads, 0.0).astype(BF)
                scores = dot(keys_twice[...], own, 1, 1) + bias[...]
                probs = jnp.exp(scores - stats_ref[2 * number + side])
                grad_probs = dot(values_twice[...], grad_own, 1, 1)
                inner = jnp.sum(probs * grad_probs, axis=0, keepdims=True)
                grad_scores = (probs * (grad_probs - inner)).astype(BF)
                key_sum[...] += dot(grad_scores, own, 1, 0)
                value_sum[...] += dot(probs.astype(BF), grad_own, 1, 0)
                parts.append(dot(keys_t[...], grad_scores, 1, 0))
            back = jnp.concatenate(parts, axis=0).T * HD ** (-0.5)
            grad_query[:, pl.ds(at, PAIR)] = turned(back, cosine, -sine).astype(BF)
            return carry

        lax.fori_loop(0, heads // 2, one_pair, 0)
        for r in range(count):
            rows = slice(r * tokens, (r + 1) * tokens)
            keys_part, values_part = key_sum[rows, :], value_sum[rows, :]
            keys_part = keys_part + pltpu.roll(keys_part, HD, 1)
            values_part = values_part + pltpu.roll(values_part, HD, 1)
            lane = lax.broadcasted_iota(jnp.int32, keys_part.shape, 1)
            outs[r][...] = jnp.where(lane < HD, keys_part, values_part).astype(BF)

    found = call(
        kernel,
        [shape((tokens, columns))] + [shape((tokens, PAIR)) for _ in blocks],
        [mid_low, query, stats] + list(tables) + list(blocks) + list(qo),
        queue,
        scratch=[
            pltpu.VMEM((total_keys, tokens), F32),
            pltpu.VMEM((total_keys, PAIR), BF),
            pltpu.VMEM((total_keys, PAIR), BF),
            pltpu.VMEM((HD, total_keys), BF),
            pltpu.VMEM((tokens, columns), BF),
            pltpu.VMEM((total_keys, PAIR), F32),
            pltpu.VMEM((total_keys, PAIR), F32),
        ],
    )
    return found[0], found[1:]


def project_back(grad_query, pieces, qo, q_at, kvg, kv_at, tables, width, queue):
    tokens, columns = grad_query.shape
    count, many = len(pieces), len(qo)
    chunks = lax.axis_size("tensor")
    layer = kvg[0]

    def kernel(place, query_ref, *refs):
        piece_refs, refs = refs[:count], refs[count:]
        qo_refs, refs = refs[:many], refs[many:]
        kv_refs, (cos_ref, sin_ref), refs = refs[:many], refs[many : many + 2], refs[many + 2 :]
        grad_pair, outs, total = refs[0], refs[1 : 1 + chunks], refs[-1]
        pair = piece_refs[0][...].astype(F32)
        for piece in piece_refs[1:]:
            pair += piece[...].astype(F32)
        pair = turned(pair, keys_only(cos_ref[...], 1.0), keys_only(-sin_ref[...], 0.0))
        grad_pair[...] = pair.astype(BF)
        for at, low, rows, feature in q_at:
            total[:, feature : feature + rows] = dot(
                query_ref[...], qo_refs[at][low : low + rows, :], 1, 1
            )
        for at, low, rows, feature in kv_at:
            total[:, feature : feature + rows] += dot(
                grad_pair[...], kv_refs[at][low : low + rows, :], 1, 1
            )
        put_chunks(place, outs, total)

    ins = [grad_query] + list(pieces) + list(qo)
    in_specs = [None] * len(ins)
    in_specs += [
        pl.BlockSpec((part.shape[0], PAIR), lambda i, place: (0, layer)) for part in kvg[1]
    ]
    in_specs += [None, None]
    found = call(
        kernel,
        [shape((tokens, PAIR))] + [shape((tokens // chunks, width)) for _ in range(chunks)],
        ins + list(kvg[1]) + list(tables),
        queue,
        in_specs=in_specs,
        scratch=[pltpu.VMEM((tokens, width), F32)],
    )
    return found[0], found[1:]


UNIT_TILE = 256


def unit_mask(tile, units, value):
    if units % UNIT_TILE == 0:
        return value
    column = tile * UNIT_TILE + lax.broadcasted_iota(jnp.int32, value.shape, 1)
    return jnp.where(column < units, value, jnp.zeros_like(value))


def joined(weights, places):
    ordered = sorted(places, key=lambda p: p[3])
    return jnp.concatenate([weights[at][low : low + rows, :] for at, low, rows, _ in ordered], axis=0)


def feed(second_in, ffn, at_of, queue):
    tokens, width = second_in.shape
    units = ffn[0].shape[1]
    many = len(ffn)
    chunks = lax.axis_size("tensor")
    steps = pl.cdiv(units, UNIT_TILE)
    gate_at, up_at, down_at = at_of

    def kernel(place, source, *refs):
        weights, refs = refs[:many], refs[many:]
        gate_ref, up_ref, hidden_ref, outs, total = refs[0], refs[1], refs[2], refs[3:-1], refs[-1]
        tile = pl.program_id(0)

        @pl.when(tile == 0)
        def _():
            total[...] = jnp.zeros_like(total)

        gate = dot(source[...], joined(weights, gate_at), 1, 0)
        up = dot(source[...], joined(weights, up_at), 1, 0)
        hidden = gate * (1.0 / (1.0 + jnp.exp(-gate))) * up
        hidden = unit_mask(tile, units, hidden).astype(BF)
        gate_ref[...] = gate.astype(BF)
        up_ref[...] = up.astype(BF)
        hidden_ref[...] = hidden
        total[...] += dot(hidden, unit_mask(tile, units, joined(weights, down_at)), 1, 1)

        @pl.when(tile == steps - 1)
        def _():
            put_chunks(place, outs, total)

    by_tile = lambda rows: pl.BlockSpec((rows, UNIT_TILE), lambda f, place: (0, f))
    found = call(
        kernel,
        [shape((tokens, units))] * 3 + [shape((tokens // chunks, width)) for _ in range(chunks)],
        [second_in] + list(ffn),
        queue,
        grid=(steps,),
        in_specs=[None] + [by_tile(part.shape[0]) for part in ffn],
        out_specs=[by_tile(tokens)] * 3 + [None] * chunks,
        scratch=[pltpu.VMEM((tokens, width), F32)],
    )
    return found[:3], found[3:]


def feed_back(grad_low, gate, up, ffn, at_of, queue):
    tokens, width = grad_low.shape
    units = gate.shape[1]
    many = len(ffn)
    chunks = lax.axis_size("tensor")
    steps = pl.cdiv(units, UNIT_TILE)
    gate_at, up_at, down_at = at_of

    def kernel(place, source, gate_ref, up_ref, *refs):
        weights, refs = refs[:many], refs[many:]
        grad_gate_ref, grad_up_ref, outs, total = refs[0], refs[1], refs[2:-1], refs[-1]
        tile = pl.program_id(0)

        @pl.when(tile == 0)
        def _():
            total[...] = jnp.zeros_like(total)

        grad_hidden = dot(source[...], joined(weights, down_at), 1, 0)
        gate, up = gate_ref[...].astype(F32), up_ref[...].astype(F32)
        sigma = 1.0 / (1.0 + jnp.exp(-gate))
        grad_gate = grad_hidden * up * sigma * (1.0 + gate * (1.0 - sigma))
        grad_up = grad_hidden * gate * sigma
        grad_gate = unit_mask(tile, units, grad_gate).astype(BF)
        grad_up = unit_mask(tile, units, grad_up).astype(BF)
        grad_gate_ref[...] = grad_gate
        grad_up_ref[...] = grad_up
        both = jnp.concatenate([grad_gate, grad_up], axis=1)
        gate_w = unit_mask(tile, units, joined(weights, gate_at))
        up_w = unit_mask(tile, units, joined(weights, up_at))
        total[...] += dot(both, jnp.concatenate([gate_w, up_w], axis=1), 1, 1)

        @pl.when(tile == steps - 1)
        def _():
            put_chunks(place, outs, total)

    by_tile = lambda rows: pl.BlockSpec((rows, UNIT_TILE), lambda f, place: (0, f))
    found = call(
        kernel,
        [shape((tokens, units))] * 2 + [shape((tokens // chunks, width)) for _ in range(chunks)],
        [grad_low, gate, up] + list(ffn),
        queue,
        grid=(steps,),
        in_specs=[None, by_tile(tokens), by_tile(tokens)] + [by_tile(p.shape[0]) for p in ffn],
        out_specs=[by_tile(tokens)] * 2 + [None] * chunks,
        scratch=[pltpu.VMEM((tokens, width), F32)],
    )
    return found[:2], found[2:]


def add_and_norm(stream, chunks, gain, queue):
    def kernel(place, stream_ref, gain_ref, *refs):
        total, normed = refs[-2:]
        values = stream_ref[...].astype(F32)
        for chunk in refs[:-2]:
            values += chunk[...].astype(F32)
        total[...] = values
        scale = lax.rsqrt(jnp.mean(values * values, axis=1, keepdims=True) + EPSILON)
        normed[...] = (values * scale * gain_ref[...]).astype(BF)

    outs = [shape(stream.shape, F32), shape(stream.shape)]
    return call(kernel, outs, [stream, gain] + list(chunks), queue)


def add_last(stream, chunks, queue):
    def kernel(place, stream_ref, *refs):
        values = stream_ref[...]
        for chunk in refs[:-1]:
            values += chunk[...].astype(F32)
        refs[-1][...] = values.astype(BF)

    return call(kernel, [shape(stream.shape)], [stream] + list(chunks), queue)[0]


def norm_back(incoming, values, gain, chunks, queue):
    def kernel(place, incoming_ref, values_ref, gain_ref, *refs):
        total, low = refs[-2:]
        grad = refs[0][...].astype(F32)
        for chunk in refs[1:-2]:
            grad += chunk[...].astype(F32)
        values = values_ref[...].astype(F32)
        scale = lax.rsqrt(jnp.mean(values * values, axis=1, keepdims=True) + EPSILON)
        unit = values * scale
        weighted = grad * gain_ref[...]
        inner = jnp.mean(weighted * unit, axis=1, keepdims=True)
        result = incoming_ref[...].astype(F32) + scale * (weighted - unit * inner)
        total[...] = result
        low[...] = result.astype(BF)

    outs = [shape(values.shape, F32), shape(values.shape)]
    ins = [incoming, values, gain] + list(chunks)
    return call(kernel, outs, ins, queue)


def weight_grads(groups, layout, block, queue):
    width = groups[0][0][0].shape[1]
    sides = width // block // 2
    tall = max(row for row, _ in layout) + block
    wide = max(col + g[1][0].shape[1] for g, (_, col) in zip(groups, layout))
    lefts, rights, left_of = [], [], []
    for left, right in groups:
        known = [k for k, other in enumerate(lefts) if other[0] is left[0]]
        left_of.append(known[0] if known else len(lefts))
        if not known:
            lefts.append(left)
        rights.append(right)
    many = len(lefts[0])
    def terms(refs):
        left_refs = [refs[k * many : (k + 1) * many] for k in range(len(lefts))]
        refs = refs[len(lefts) * many :]
        right_refs = [refs[k * many : (k + 1) * many] for k in range(len(rights))]
        left_all = [jnp.concatenate([x[...] for x in group], axis=0).T for group in left_refs]
        found = []
        for k, group in enumerate(right_refs):
            right = jnp.concatenate([x[...] for x in group], axis=0)
            found.append(dot(left_all[left_of[k]], right, 1, 0))
        return found

    ins = [x for left in lefts for x in left] + [x for right in rights for x in right]
    read = len(ins)

    def specs(first):
        tokens = lefts[0][0].shape[0]
        cut = pl.BlockSpec((tokens, block), lambda i, place: (0, first + i))
        return [cut] * (len(lefts) * many) + [None] * (len(rights) * many)

    def send_kernel(place, *refs):
        for value, (row, col), group in zip(terms(refs[:read]), layout, groups):
            columns = group[1][0].shape[1]
            refs[-1][row : row + block, col : col + columns] = value.astype(BF)

    row_block = pl.BlockSpec((tall, wide), lambda i, place: (i, 0))
    send = call(
        send_kernel,
        [shape((sides * tall, wide))],
        ins,
        queue,
        grid=(sides,),
        in_specs=specs(sides),
        out_specs=[row_block],
    )[0]
    got = swap(send, "dp", 1)
    half = tall // 2
    yield None
    if sides != 4:
        keep = call(
            send_kernel,
            [shape((sides * tall, wide))],
            ins,
            queue,
            grid=(sides,),
            in_specs=specs(0),
            out_specs=[row_block],
        )[0]
        both = keep.astype(F32) + got.astype(F32)
        bit = sides // 2
        while bit:
            middle = both.shape[0] // 2
            both = both[:middle] + swap(both[middle:].astype(BF), "context", bit).astype(F32)
            bit //= 2
        yield None
        none = jnp.zeros_like(both[:half])
        yield [both[:half], none, both[half:], none]
        return

    def keep_kernel(place, *refs):
        got_ref = refs[read]
        low_keep, low_send, high_keep, high_send = refs[read + 1 :]
        step = pl.program_id(0)
        found = terms(refs[:read])

        def write(target, start):
            for value, (row, col), group in zip(found, layout, groups):
                columns = slice(col, col + group[1][0].shape[1])
                first, last = max(row, start), min(row + block, start + half)
                if first < last:
                    target[first - start : last - start, columns] = (
                        value[first - row : last - row] + got_ref[first:last, columns].astype(F32)
                    ).astype(BF)

        for number, (low, high) in enumerate(
            ((low_keep, high_keep), (low_send, high_keep), (low_keep, high_send), (low_send, high_send))
        ):
            @pl.when(step == number)
            def _(low=low, high=high):
                write(low, 0)
                write(high, half)

    piece = lambda index: pl.BlockSpec((half, wide), index)
    low_keep, low_send, high_keep, high_send = call(
        keep_kernel,
        [shape((tall, wide))] * 4,
        ins + [got],
        queue,
        grid=(sides,),
        in_specs=specs(0) + [row_block],
        out_specs=[
            piece(lambda i, place: (i // 2, 0)),
            piece(lambda i, place: (i // 3, 0)),
            piece(lambda i, place: (jnp.minimum(i, 1), 0)),
            piece(lambda i, place: (i // 3, 0)),
        ],
    )
    low_got = swap(low_send, "context", 1)
    high_got = swap(high_send, "context", 2)
    yield None

    def fold(place, a, b, c, d, low_own, low_next, high_own, high_next):
        for first, second, own, next_ref in ((a, b, low_own, low_next), (c, d, high_own, high_next)):
            both = first[...].astype(F32) + second[...].astype(F32)
            own[...] = both[:half].astype(BF)
            next_ref[...] = both[half:].astype(BF)

    columns = PAIR if wide % PAIR == 0 else wide
    by_columns = lambda rows: pl.BlockSpec((rows, columns), lambda i, place: (0, i))
    low_own, low_next, high_own, high_next = call(
        fold,
        [shape((half, wide))] * 4,
        [low_keep, low_got, high_keep, high_got],
        queue,
        grid=(wide // columns,),
        in_specs=[by_columns(tall)] * 4,
        out_specs=[by_columns(half)] * 4,
    )
    yield [low_own, swap(low_next, "context", 2), high_own, swap(high_next, "context", 1)]


def finish_ffn(parts, gate_w, up_w, queue):
    block, units = gate_w.shape
    half = parts[0].shape[0]

    def kernel(place, a, b, c, d, gate_ref, up_ref, gate_out, up_out, down_out, sums):
        def part(first, last):
            found = []
            for start, x, y in ((0, a, b), (half, c, d)):
                low, high = max(first, start), min(last, start + half)
                if low < high:
                    rows = slice(low - start, high - start)
                    found.append(x[rows, :].astype(F32) + y[rows, :].astype(F32))
            return jnp.concatenate(found, axis=0)

        gate_out[...] = part(0, block)
        up_out[...] = part(block, 2 * block)
        down_out[...] = part(2 * block, 3 * block)
        product = gate_out[...] * gate_ref[...].astype(F32) + up_out[...] * up_ref[...].astype(F32)
        sums[...] = jnp.broadcast_to(jnp.sum(product, axis=1, keepdims=True), sums.shape)

    outs = [shape((block, units), F32)] * 3 + [shape((block, PAIR), F32)]
    return call(kernel, outs, list(parts) + [gate_w, up_w], queue)


def finish_heads(parts, query_w, pair_w, queue):
    block, columns = query_w.shape
    half = parts[0].shape[0]

    def kernel(place, a, b, c, d, query_ref, pair_ref, query_out, output_out, pair_out, sums):
        for start, x, y in ((0, a, b), (half, c, d)):
            both = x[...].astype(F32) + y[...].astype(F32)
            rows = slice(start, start + half)
            query_out[rows, :] = both[:, :columns]
            output_out[rows, :] = both[:, columns : 2 * columns]
            pair_out[rows, :] = both[:, 2 * columns :]
        total = jnp.sum(query_out[...] * query_ref[...].astype(F32), axis=1, keepdims=True)
        total += jnp.sum(pair_out[...] * pair_ref[...].astype(F32), axis=1, keepdims=True)
        sums[...] = jnp.broadcast_to(total, sums.shape)

    outs = [shape((block, columns), F32)] * 2 + [shape((block, PAIR), F32)] * 2
    return call(kernel, outs, list(parts) + [query_w, pair_w], queue)


def per_device(hidden_input, cotangent, *params):
    layers = (params[:9], params[9:])
    tensor_count = lax.axis_size("tensor")
    context_count = lax.axis_size("context")
    sequences, _, rows, width = hidden_input.shape
    tokens = rows * tensor_count
    block = layers[0][1].shape[0]
    query_width = layers[0][1].shape[1]
    heads = query_width // HD
    heads_of = [j * heads // (H // KV) for j in range(tensor_count)]
    context = lax.axis_index("context")
    place = jnp.stack(
        [lax.axis_index("dp") * context_count + context, context, lax.axis_index("tensor")]
    ).astype(jnp.int32)
    streams = range(sequences)

    positions = context * tokens + jnp.arange(tokens, dtype=jnp.int32)
    freq = THETA ** (-2.0 * jnp.arange(HD // 2, dtype=F32) / HD)
    angle = positions.astype(F32)[:, None] * freq[None, :]
    cosine, sine = jnp.cos(angle), jnp.sin(angle)
    tables = (
        jnp.concatenate([cosine] * 4, axis=1),
        jnp.concatenate([-sine, sine] * 2, axis=1),
    )

    queue = Queue(place)

    me = lax.axis_index("tensor")
    gains = jnp.stack([layers[0][0], layers[0][5], layers[1][0], layers[1][5]], axis=1)
    gains = jnp.pad(gains, ((0, 0), (0, PAIR - 4)))
    wide_w = [w for layer in layers for w in (layer[2], layer[3])]
    small = []
    for k in range(tensor_count):
        head = ((me ^ k) * heads) // (H // KV)
        cut = [lax.dynamic_slice_in_dim(w, head * HD, HD, 1) for w in wide_w]
        piece = jnp.concatenate(cut + [gains], axis=1)
        small.append(swap(piece, "tensor", k) if k else piece)

    moved = reorder([hidden_input[i, 0] for i in streams] + [cotangent[i, 0] for i in streams], queue)
    first_low, incoming = moved[:sequences], moved[sequences:]
    normed = [[gather_tokens(low)] for low in first_low]
    grad_all = [gather_tokens(low) for low in incoming]

    stack_qo = lambda layer: gather_near(stacked([layer[1], layer[4]], queue))
    stack_ffn = lambda layer: gather_near(stacked([layer[6], layer[7], layer[8]], queue))
    qo_of, ffn_of = [stack_qo(layers[0]), None], [None, None]
    small = placed(small, queue)
    kvg = gather_near(small)
    qo_of[0] = gather_far(qo_of[0], queue)
    kvg = gather_far(kvg, queue)
    pairs_w = (small[:, :PAIR], small[:, PAIR : 2 * PAIR])
    gain_rows = small[:, 2 * PAIR :]
    kv_at = segments(kvg, 0, block, block)
    q_at = segments(qo_of[0], 0, block, block)
    o_at = segments(qo_of[0], block, 2 * block, block)
    gain_all = gain_vectors(kvg, kv_at, width, queue)
    gain_of = lambda number, part: gain_all[2 * number + part : 2 * number + part + 1]

    saved = [[{}, {}] for _ in streams]
    state = list(first_low)
    chunks = [None for _ in streams]

    def enter(number, i):
        keep = saved[i][number]
        keep["stream"] = state[i]
        gain = gain_of(0, 0) if number == 0 else None
        keep["query"], pair, keep["first_in"] = project(
            normed[i], gain, qo_of[number], q_at, (number, kvg), kv_at, tables, queue
        )
        keep["blocks"] = exchange_blocks([pair] * context_count)

    def mix(number, i):
        keep = saved[i][number]
        keep["mixed"], keep["stats"], out = attend(
            keep["query"], keep["blocks"], qo_of[number], o_at, number == 0, width, queue
        )
        chunks[i] = exchange_tokens(out)

    def between(number, i):
        keep = saved[i][number]
        keep["middle"], low = add_and_norm(state[i], chunks[i], gain_of(number, 1), queue)
        keep["second_in"] = gather_tokens(low)

    def forward_units(number, i):
        keep = saved[i][number]
        (keep["gate"], keep["up"], keep["hidden"]), out = feed(
            keep["second_in"], ffn_of[number], ffn_at, queue
        )
        chunks[i] = exchange_tokens(out)

    first, last = 0, sequences - 1
    for i in streams:
        enter(0, i)
        mix(0, i)
    queue.due = [x for i in streams for x in saved[i][0]["blocks"]] + [grad_all[0]]
    ffn_of[0] = stack_ffn(layers[0])
    between(0, 0)
    ffn_of[0] = gather_far(ffn_of[0], queue)
    ffn_at = [segments(ffn_of[0], k * block, (k + 1) * block, block) for k in range(3)]
    qo_of[1] = stack_qo(layers[1])
    for i in streams[1:]:
        between(0, i)
    for i in streams:
        forward_units(0, i)
        if i == 0:
            qo_of[1] = gather_far(qo_of[1], queue)
            ffn_of[1] = stack_ffn(layers[1])
    for i in streams:
        state[i], low = add_and_norm(saved[i][0]["middle"], chunks[i], gain_of(1, 0), queue)
        normed[i] = [gather_tokens(low)]
    for i in streams:
        enter(1, i)
        mix(1, i)
    queue.due = [x for i in streams for x in saved[i][1]["blocks"]]
    ffn_of[1] = gather_far(ffn_of[1], queue)
    for i in streams:
        if i == last:
            queue.due = list(ffn_of[1])
        between(1, i)
    for i in streams:
        forward_units(1, i)

    last_chunks = list(chunks)
    ffn_work, head_work = [None, None], [None, None]
    summed = [None, None]

    def add_out(i):
        state[i] = add_last(saved[i][1]["middle"], last_chunks[i], queue)

    def back_units(number, i):
        keep = saved[i][number]
        keep["grad_all"] = grad_all[i]
        (keep["grad_gate"], keep["grad_up"]), out = feed_back(
            grad_all[i], keep["gate"], keep["up"], ffn_of[number], ffn_at, queue
        )
        chunks[i] = exchange_tokens(out)

    def back_between(number, i):
        keep = saved[i][number]
        keep["grad_mid"], low = norm_back(
            incoming[i], keep["middle"], gain_of(number, 1), chunks[i], queue
        )
        keep["mid_all"] = gather_tokens(low)

    pieces = [None for _ in streams]

    def back_mix(number, i):
        keep = saved[i][number]
        keep["grad_query"], pieces[i] = attend_back(
            keep["mid_all"], keep["query"], keep["blocks"], keep["stats"], qo_of[number], o_at,
            tables, number == 0, queue,
        )
        pieces[i] = exchange_blocks(pieces[i])

    def back_enter(number, i):
        keep = saved[i][number]
        keep["grad_pair"], out = project_back(
            keep["grad_query"], pieces[i], qo_of[number], q_at, (number, kvg), kv_at, tables,
            width, queue,
        )
        chunks[i] = exchange_tokens(out)

    def leave(number, i):
        keep = saved[i][number]
        incoming[i], low = norm_back(
            keep["grad_mid"], keep["stream"], gain_of(number, 0), chunks[i], queue
        )
        if number == 1:
            grad_all[i] = gather_tokens(low)

    def ffn_grads(number):
        both = lambda name: tuple(saved[i][number][name] for i in streams)
        ffn_work[number] = weight_grads(
            [
                (both("second_in"), both("grad_gate")),
                (both("second_in"), both("grad_up")),
                (both("grad_all"), both("hidden")),
            ],
            [(0, 0), (block, 0), (2 * block, 0)],
            block,
            queue,
        )
        next(ffn_work[number])

    def head_grads(number):
        both = lambda name: tuple(saved[i][number][name] for i in streams)
        head_work[number] = weight_grads(
            [
                (both("first_in"), both("grad_query")),
                (both("mid_all"), both("mixed")),
                (both("first_in"), both("grad_pair")),
            ],
            [(0, 0), (0, query_width), (0, 2 * query_width)],
            block,
            queue,
        )
        next(head_work[number])

    def fold_ffn(number):
        summed[number] = [next(ffn_work[number]), None]

    def fold_heads(number):
        summed[number][1] = next(head_work[number])

    def end_ffn(number):
        layer = layers[number]
        summed[number][0] = finish_ffn(summed[number][0], layer[6], layer[7], queue)

    def end_heads(number):
        summed[number][1] = finish_heads(
            summed[number][1], layers[number][1], pairs_w[number], queue
        )

    for i in streams:
        back_units(1, i)
        if i == 0:
            add_out(0)
    ffn_grads(1)
    for i in streams:
        back_between(1, i)
    for i in streams:
        back_mix(1, i)
    for i in streams[1:]:
        add_out(i)
    next(ffn_work[1])
    for i in streams:
        back_enter(1, i)
    head_grads(1)
    next(head_work[1])
    for i in streams:
        leave(1, i)
    fold_ffn(1)
    fold_heads(1)
    for i in streams:
        back_units(0, i)
    end_ffn(1)
    end_heads(1)
    ffn_grads(0)
    back_between(0, 0)
    next(ffn_work[0])
    for i in streams[1:]:
        back_between(0, i)
    for i in streams:
        back_mix(0, i)
    fold_ffn(0)
    for i in streams:
        back_enter(0, i)
    head_grads(0)
    next(head_work[0])
    end_ffn(0)
    for i in streams:
        leave(0, i)
    fold_heads(0)
    outputs = jnp.stack(reorder(state, queue))
    in_grads = jnp.stack(reorder(incoming, queue))
    end_heads(0)

    sums = []
    for number in range(2):
        own_gains = gain_rows[:, 2 * number : 2 * number + 2].astype(F32)
        sums.append(summed[number][1][3][:, :1] / own_gains[:, :1])
        sums.append(summed[number][0][3][:, :1] / own_gains[:, 1:])
    tail = jnp.pad(jnp.concatenate(sums, axis=1), ((0, 0), (0, PAIR - 4)))
    small_g = lax.all_to_all(
        jnp.concatenate([summed[0][1][2], summed[1][1][2], tail], axis=1),
        "tensor", split_axis=0, concat_axis=0, tiled=True,
    ).reshape(tensor_count, -1, 3 * PAIR)
    gain_g = jnp.sum(small_g[:, :, 2 * PAIR : 2 * PAIR + 4], axis=0)

    results = [
        outputs.reshape(hidden_input.shape),
        in_grads.reshape(hidden_input.shape),
    ]
    for number in range(2):
        ffn_g, head_g = summed[number]
        pair_g = []
        for part in range(2):
            at = (2 * number + part) * HD
            by_head = []
            for head in range(KV):
                pieces = [
                    small_g[j, :, at : at + HD] for j in range(tensor_count) if heads_of[j] == head
                ]
                by_head.append(sum(pieces))
            pair_g.append(jnp.concatenate(by_head, axis=1))
        results += [
            gain_g[:, 2 * number],
            head_g[0],
            pair_g[0],
            pair_g[1],
            head_g[1],
            gain_g[:, 2 * number + 1],
            ffn_g[0],
            ffn_g[1],
            ffn_g[2],
        ]
    return tuple(results)


def solution(mesh):
    rows = P(("dp", "context", "tensor"))
    tall = P(("dp", "context", "tensor"), None)
    wide = P(("dp", "context"), "tensor")
    tokens = P(None, "dp", ("context", "tensor"), None)
    layer = (rows, wide, tall, tall, wide, rows, wide, wide, wide)
    return jax.shard_map(
        per_device,
        mesh=mesh,
        in_specs=(tokens, tokens) + layer + layer,
        out_specs=(tokens, tokens) + layer + layer,
        check_vma=False,
    )
```

```python
import functools

import jax
import jax.numpy as jnp
from jax import lax
from jax.experimental import pallas as pl
from jax.experimental.pallas import tpu as pltpu
from jax.sharding import PartitionSpec as P

H = 32
KV = 4
HD = 64
WINDOW = 512
EPSILON = 1e-05
THETA = 10000.0
NEGATIVE = -1e30
BF = jnp.bfloat16
F32 = jnp.float32
PAIR = 2 * HD
COST = {
    "project": 5.0,
    "attend": 12.0,
    "attend_back": 13.0,
    "project_back": 5.0,
    "feed": 13.0,
    "feed_back": 15.0,
    "weights": 6.0,
    "fold": 3.0,
    "finish_ffn": 6.0,
    "stacked": 4.0,
}
WEIGHT = 3.0e6
VMEM_LIMIT = 60 * 1024 * 1024


def swap(value, axis, bits):
    count = lax.axis_size(axis)
    return lax.ppermute(value, axis, [(source, source ^ bits) for source in range(count)])


def gather_near(stack):
    if lax.axis_size("context") != 4:
        return [stack]
    return [stack, swap(stack, "context", 1), swap(stack, "context", 2)]


def gather_far(parts, queue, due=()):
    count = lax.axis_size("context")
    if count == 4:
        loose = Queue(queue.place)
        loose.due = list(due)
        low, high = halves(parts[2], parts[1], loose)
        parts = parts + [swap(low, "context", 1), swap(high, "context", 2)]
    else:
        bit = 1
        while bit < count:
            parts = parts + [swap(part, "context", bit) for part in parts]
            bit *= 2
    return parts + [swap(part, "dp", 1) for part in parts]


def segments(parts, low, high, block):
    found = []
    side = len(parts) // 2
    full = parts[0].shape[0]
    for core in range(2):
        feature = core * (side - (1 if side == 5 else 0)) * block
        for number in range(side):
            at = core * side + number
            if side == 5 and number >= 3:
                cut = full // 2
                start, stop = (0, cut) if number == 3 else (cut, full)
                first, last = max(low, start), min(high, stop)
                if first < last:
                    found.append((at, first - start, last - first, feature + 3 * block + first - low))
            else:
                found.append((at, low, high - low, feature + number * block))
    return found


def gather_tokens(piece):
    return lax.all_gather(piece, "tensor", axis=0, tiled=True)


def exchange_tokens(chunks):
    return [lax.all_to_all(chunks[0], "tensor", split_axis=0, concat_axis=0, tiled=True)]


def exchange_blocks(pieces):
    return [pieces[0]] + [swap(pieces[r], "context", r) for r in range(1, len(pieces))]


def dot(left, right, left_dim, right_dim):
    return lax.dot_general(
        left, right, (((left_dim,), (right_dim,)), ((), ())), preferred_element_type=F32
    )


class Queue:
    def __init__(self, place):
        self.place = place
        self.last = None
        self.due = []


def call(kernel, outs, ins, queue, grid=(1,), in_specs=None, out_specs=None, scratch=()):
    whole = lambda x: pl.BlockSpec(x.shape, lambda *i, n=len(x.shape): (0,) * n)
    in_specs = [whole(x) if s is None else s for x, s in zip(ins, in_specs or [None] * len(ins))]
    out_specs = [whole(x) if s is None else s for x, s in zip(outs, out_specs or [None] * len(outs))]
    before = [x for x in [queue.last] + queue.due if x is not None]
    queue.due = []
    count = len(ins)
    name = kernel.__qualname__.split(".")[0]
    if name == "weight_grads":
        name = kernel.__qualname__.split(".")[-1]

    def ordered(place, *refs):
        kernel(place, *refs[:count], *refs[count + len(before) :])

    found = list(pl.pallas_call(
        ordered,
        name=name,
        out_shape=outs,
        grid_spec=pltpu.PrefetchScalarGridSpec(
            num_scalar_prefetch=1,
            grid=grid,
            in_specs=in_specs + [pl.BlockSpec(memory_space=pl.ANY)] * len(before),
            out_specs=out_specs,
            scratch_shapes=list(scratch),
        ),
        compiler_params=pltpu.CompilerParams(
            vmem_limit_bytes=VMEM_LIMIT, dimension_semantics=("arbitrary",) * len(grid)
        ),
        cost_estimate=pl.CostEstimate(
            flops=int(COST.get(name, 3.0) * 0.2 * 1.0e9), bytes_accessed=int(COST.get(name, 3.0) * 1 * 3.0e6), transcendentals=0
        ),
    )(queue.place, *ins, *before))
    queue.last = min(found, key=lambda x: x.size)
    return found


def shape(dims, dtype=BF):
    return jax.ShapeDtypeStruct(dims, dtype)


def stacked(pieces, place, due=()):
    queue = Queue(place)
    queue.due = list(due)
    rows, columns = pieces[0].shape

    def kernel(place, *refs):
        for number, source in enumerate(refs[:-1]):
            @pl.when(pl.program_id(0) == number)
            def _(source=source):
                refs[-1][...] = source[...]

    return call(
        kernel,
        [shape((len(pieces) * rows, columns))],
        pieces,
        queue,
        grid=(len(pieces),),
        out_specs=[pl.BlockSpec((rows, columns), lambda i, place: (i, 0))],
    )[0]


def halves(first, second, queue):
    rows, columns = first.shape
    half = rows // 2

    def kernel(place, first_ref, second_ref, upper, lower):
        upper[...] = first_ref[...]
        lower[...] = second_ref[...]

    return call(
        kernel,
        [shape((half, columns))] * 2,
        [first, second],
        queue,
        in_specs=[
            pl.BlockSpec((half, columns), lambda i, place: (0, 0)),
            pl.BlockSpec((half, columns), lambda i, place: (1, 0)),
        ],
    )


def placed(pieces, queue):
    rows, columns = pieces[0].shape

    def kernel(place, *refs):
        for k, source in enumerate(refs[:-1]):
            at = pl.multiple_of((place[2] ^ k) * rows, rows)
            refs[-1][pl.ds(at, rows), :] = source[...]

    return call(kernel, [shape((len(pieces) * rows, columns))], pieces, queue)[0]


def gain_vectors(kvg, kv_at, width, queue):
    def kernel(place, *refs):
        row = lax.broadcasted_iota(jnp.int32, (8, PAIR), 0)
        pick = (row == lax.broadcasted_iota(jnp.int32, (8, PAIR), 1)).astype(BF)
        for at, low, rows, feature in kv_at:
            refs[-1][:, feature : feature + rows] = dot(pick, refs[at][low : low + rows, :], 1, 1)

    return call(
        kernel,
        [shape((8, width), F32)],
        kvg,
        queue,
        in_specs=[pl.BlockSpec((p.shape[0], PAIR), lambda i, place: (0, 2)) for p in kvg],
    )[0]


def reorder(pieces, queue):
    width = pieces[0].shape[-1]
    count = 2 * lax.axis_size("context")
    block = width // count

    def kernel(place, *refs):
        for source, target in zip(refs[: len(pieces)], refs[len(pieces) :]):
            for r in range(count):
                at = pl.multiple_of((place[0] ^ r) * block, block)
                target[:, r * block : (r + 1) * block] = source[:, pl.ds(at, block)]

    return call(kernel, [shape(p.shape, p.dtype) for p in pieces], pieces, queue)


def turned(tile, cosine, sine):
    lane = lax.broadcasted_iota(jnp.int32, tile.shape, 1)
    half = HD // 2
    other = jnp.where(
        lane % HD < half, pltpu.roll(tile, PAIR - half, 1), pltpu.roll(tile, half, 1)
    )
    return tile * cosine + other * sine


def keys_only(table, fill):
    lane = lax.broadcasted_iota(jnp.int32, table.shape, 1)
    return jnp.where(lane < HD, table, fill)


def put_chunks(place, outs, total):
    outs[0][...] = total[...].astype(BF)


def project(sources, gain, qo, qo_at, kvg, kv_at, tables, queue):
    piece_rows, width = sources[0].shape
    tokens = piece_rows * len(sources)
    columns = qo[0].shape[1]
    raw = gain is not None
    count = len(qo)

    def kernel(place, *refs):
        if raw:
            refs, (query, pair, normed) = refs[:-3], refs[-3:]
            gain_ref, refs = refs[0], refs[1:]
        else:
            refs, (query, pair) = refs[:-2], refs[-2:]
        source_refs, refs = refs[: len(sources)], refs[len(sources) :]
        source = source_refs[0]
        qo_refs, kv_refs, (cos_ref, sin_ref) = refs[:count], refs[count:-2], refs[-2:]
        if raw:
            for k, piece in enumerate(source_refs):
                values = piece[...].astype(F32)
                scale = lax.rsqrt(jnp.mean(values * values, axis=1, keepdims=True) + EPSILON)
                at = 0
                if len(sources) > 1:
                    at = pl.multiple_of((place[2] ^ k) * piece_rows, piece_rows)
                normed[pl.ds(at, piece_rows), :] = (values * scale * gain_ref[...]).astype(BF)
            source = normed
        cosine, sine = cos_ref[...], sin_ref[...]
        pre = 0.0
        for at, low, rows, feature in qo_at:
            pre += dot(source[:, feature : feature + rows], qo_refs[at][low : low + rows, :], 1, 0)
        for tile in range(columns // PAIR):
            part = slice(tile * PAIR, (tile + 1) * PAIR)
            query[:, part] = turned(pre[:, part], cosine, sine).astype(BF)
        pre = 0.0
        for at, low, rows, feature in kv_at:
            pre += dot(source[:, feature : feature + rows], kv_refs[at][low : low + rows, :], 1, 0)
        pair[...] = turned(pre, keys_only(cosine, 1.0), keys_only(sine, 0.0)).astype(BF)

    outs = [shape((tokens, columns)), shape((tokens, PAIR))]
    if raw:
        outs.append(shape((tokens, width)))
    ins = ([gain] if raw else []) + list(sources) + list(qo) + list(kvg[1]) + list(tables)
    layer = kvg[0]
    in_specs = [None] * (len(ins) - len(kvg[1]) - 2)
    in_specs += [
        pl.BlockSpec((part.shape[0], PAIR), lambda i, place: (0, layer)) for part in kvg[1]
    ]
    in_specs += [None, None]
    found = call(
        kernel,
        outs,
        ins,
        queue,
        in_specs=in_specs,
    )
    return found if raw else found + [sources[0]]


def mask_bias(place, bias, tokens, blocks, is_window):
    query_pos = place[1] * tokens + lax.broadcasted_iota(jnp.int32, (tokens, tokens), 1)
    key_row = lax.broadcasted_iota(jnp.int32, (tokens, tokens), 0)
    for r in range(blocks):
        key_pos = (place[1] ^ r) * tokens + key_row
        allowed = key_pos <= query_pos
        if is_window:
            allowed = allowed & (query_pos - key_pos < WINDOW)
        bias[r * tokens : (r + 1) * tokens, :] = jnp.where(allowed, 0.0, NEGATIVE)


def head_masks(tokens):
    lane = lax.broadcasted_iota(jnp.int32, (tokens, PAIR), 1)
    return (lane < HD, lane >= HD)


def attend(query, blocks, qo, o_at, is_window, width, queue):
    tokens, columns = query.shape
    heads = columns // HD
    count, many = len(blocks), len(qo)
    total_keys = count * tokens
    chunks = 1

    def kernel(place, query_ref, *refs):
        block_refs, refs = refs[:count], refs[count:]
        qo_refs, refs = refs[:many], refs[many:]
        mixed, stats, refs = refs[0], refs[1], refs[2:]
        outs, (bias, keys_twice, values_t, total) = refs[:chunks], refs[chunks:]
        mask_bias(place, bias, tokens, count, is_window)
        for r in range(count):
            rows = slice(r * tokens, (r + 1) * tokens)
            both = block_refs[r][...].astype(F32)
            first = keys_only(both, 0.0)
            keys_twice[rows, :] = (first + pltpu.roll(first, HD, 1)).astype(BF)
            values_t[:, rows] = pltpu.roll(both, HD, 1).T[:HD, :].astype(BF)
        masks = head_masks(tokens)

        def one_pair(number, carry):
            at = pl.multiple_of(number * PAIR, PAIR)
            queries = query_ref[:, pl.ds(at, PAIR)].astype(F32) * HD ** (-0.5)
            parts = []
            for side in range(2):
                own = jnp.where(masks[side], queries, 0.0).astype(BF)
                scores = dot(keys_twice[...], own, 1, 1) + bias[...]
                top = jnp.max(scores, axis=0, keepdims=True)
                expo = jnp.exp(scores - top)
                amount = jnp.sum(expo, axis=0, keepdims=True)
                parts.append(dot(values_t[...], expo.astype(BF), 1, 0) * (1.0 / amount))
                stats[2 * number + side] = top + jnp.log(amount)
            mixed[:, pl.ds(at, PAIR)] = jnp.concatenate(parts, axis=0).T.astype(BF)
            return carry

        lax.fori_loop(0, heads // 2, one_pair, 0)
        for at, low, rows, feature in o_at:
            total[:, feature : feature + rows] = dot(
                mixed[...], qo_refs[at][low : low + rows, :], 1, 1
            )
        put_chunks(place, outs, total)

    outs = [shape((tokens, columns)), shape((heads, 1, tokens), F32)]
    outs += [shape((tokens // chunks, width)) for _ in range(chunks)]
    found = call(
        kernel,
        outs,
        [query] + list(blocks) + list(qo),
        queue,
        scratch=[
            pltpu.VMEM((total_keys, tokens), F32),
            pltpu.VMEM((total_keys, PAIR), BF),
            pltpu.VMEM((HD, total_keys), BF),
            pltpu.VMEM((tokens, width), F32),
        ],
    )
    return found[0], found[1], found[2:]


def attend_back(mid_low, query, blocks, stats, qo, o_at, tables, is_window, queue):
    tokens, columns = query.shape
    width = mid_low.shape[1]
    heads = columns // HD
    count, many = len(blocks), len(qo)
    total_keys = count * tokens

    def kernel(place, mid_ref, query_ref, stats_ref, cos_ref, sin_ref, *refs):
        block_refs, refs = refs[:count], refs[count:]
        qo_refs, refs = refs[:many], refs[many:]
        grad_query, refs = refs[0], refs[1:]
        outs, refs = refs[:count], refs[count:]
        bias, keys_twice, values_twice, keys_t, grad_mixed, key_sum, value_sum = refs
        pre = 0.0
        for at, low, rows, feature in o_at:
            pre += dot(mid_ref[:, feature : feature + rows], qo_refs[at][low : low + rows, :], 1, 0)
        grad_mixed[...] = pre.astype(BF)
        mask_bias(place, bias, tokens, count, is_window)
        for r in range(count):
            rows = slice(r * tokens, (r + 1) * tokens)
            both = block_refs[r][...].astype(F32)
            first = keys_only(both, 0.0)
            last = both - first
            keys_twice[rows, :] = (first + pltpu.roll(first, HD, 1)).astype(BF)
            values_twice[rows, :] = (last + pltpu.roll(last, HD, 1)).astype(BF)
            keys_t[:, rows] = both.T[:HD, :].astype(BF)
        key_sum[...] = jnp.zeros_like(key_sum)
        value_sum[...] = jnp.zeros_like(value_sum)
        masks = head_masks(tokens)
        cosine, sine = cos_ref[...], sin_ref[...]

        def one_pair(number, carry):
            at = pl.multiple_of(number * PAIR, PAIR)
            queries = query_ref[:, pl.ds(at, PAIR)].astype(F32) * HD ** (-0.5)
            grads = grad_mixed[:, pl.ds(at, PAIR)].astype(F32)
            parts = []
            for side in range(2):
                own = jnp.where(masks[side], queries, 0.0).astype(BF)
                grad_own = jnp.where(masks[side], grads, 0.0).astype(BF)
                scores = dot(keys_twice[...], own, 1, 1) + bias[...]
                probs = jnp.exp(scores - stats_ref[2 * number + side])
                grad_probs = dot(values_twice[...], grad_own, 1, 1)
                inner = jnp.sum(probs * grad_probs, axis=0, keepdims=True)
                grad_scores = (probs * (grad_probs - inner)).astype(BF)
                key_sum[...] += dot(grad_scores, own, 1, 0)
                value_sum[...] += dot(probs.astype(BF), grad_own, 1, 0)
                parts.append(dot(keys_t[...], grad_scores, 1, 0))
            back = jnp.concatenate(parts, axis=0).T * HD ** (-0.5)
            grad_query[:, pl.ds(at, PAIR)] = turned(back, cosine, -sine).astype(BF)
            return carry

        lax.fori_loop(0, heads // 2, one_pair, 0)
        for r in range(count):
            rows = slice(r * tokens, (r + 1) * tokens)
            keys_part, values_part = key_sum[rows, :], value_sum[rows, :]
            keys_part = keys_part + pltpu.roll(keys_part, HD, 1)
            values_part = values_part + pltpu.roll(values_part, HD, 1)
            lane = lax.broadcasted_iota(jnp.int32, keys_part.shape, 1)
            outs[r][...] = jnp.where(lane < HD, keys_part, values_part).astype(BF)

    found = call(
        kernel,
        [shape((tokens, columns))] + [shape((tokens, PAIR)) for _ in blocks],
        [mid_low, query, stats] + list(tables) + list(blocks) + list(qo),
        queue,
        scratch=[
            pltpu.VMEM((total_keys, tokens), F32),
            pltpu.VMEM((total_keys, PAIR), BF),
            pltpu.VMEM((total_keys, PAIR), BF),
            pltpu.VMEM((HD, total_keys), BF),
            pltpu.VMEM((tokens, columns), BF),
            pltpu.VMEM((total_keys, PAIR), F32),
            pltpu.VMEM((total_keys, PAIR), F32),
        ],
    )
    return found[0], found[1:]


def project_back(grad_query, pieces, qo, q_at, kvg, kv_at, tables, width, queue):
    tokens, columns = grad_query.shape
    count, many = len(pieces), len(qo)
    chunks = 1
    layer = kvg[0]

    def kernel(place, query_ref, *refs):
        piece_refs, refs = refs[:count], refs[count:]
        qo_refs, refs = refs[:many], refs[many:]
        kv_refs, (cos_ref, sin_ref), refs = refs[:many], refs[many : many + 2], refs[many + 2 :]
        grad_pair, outs, total = refs[0], refs[1 : 1 + chunks], refs[-1]
        pair = piece_refs[0][...].astype(F32)
        for piece in piece_refs[1:]:
            pair += piece[...].astype(F32)
        pair = turned(pair, keys_only(cos_ref[...], 1.0), keys_only(-sin_ref[...], 0.0))
        grad_pair[...] = pair.astype(BF)
        for at, low, rows, feature in q_at:
            total[:, feature : feature + rows] = dot(
                query_ref[...], qo_refs[at][low : low + rows, :], 1, 1
            )
        for at, low, rows, feature in kv_at:
            total[:, feature : feature + rows] += dot(
                grad_pair[...], kv_refs[at][low : low + rows, :], 1, 1
            )
        put_chunks(place, outs, total)

    ins = [grad_query] + list(pieces) + list(qo)
    in_specs = [None] * len(ins)
    in_specs += [
        pl.BlockSpec((part.shape[0], PAIR), lambda i, place: (0, layer)) for part in kvg[1]
    ]
    in_specs += [None, None]
    found = call(
        kernel,
        [shape((tokens, PAIR))] + [shape((tokens // chunks, width)) for _ in range(chunks)],
        ins + list(kvg[1]) + list(tables),
        queue,
        in_specs=in_specs,
        scratch=[pltpu.VMEM((tokens, width), F32)],
    )
    return found[0], found[1:]


UNIT_TILE = 256


def unit_mask(tile, units, value):
    if units % UNIT_TILE == 0:
        return value
    column = tile * UNIT_TILE + lax.broadcasted_iota(jnp.int32, value.shape, 1)
    return jnp.where(column < units, value, jnp.zeros_like(value))


def joined(weights, places):
    ordered = sorted(places, key=lambda p: p[3])
    return jnp.concatenate([weights[at][low : low + rows, :] for at, low, rows, _ in ordered], axis=0)


def feed(second_in, ffn, at_of, queue):
    tokens, width = second_in.shape
    units = ffn[0].shape[1]
    many = len(ffn)
    chunks = 1
    steps = pl.cdiv(units, UNIT_TILE)
    gate_at, up_at, down_at = at_of

    def kernel(place, source, *refs):
        weights, refs = refs[:many], refs[many:]
        gate_ref, up_ref, hidden_ref, outs, total = refs[0], refs[1], refs[2], refs[3:-1], refs[-1]
        tile = pl.program_id(0)

        @pl.when(tile == 0)
        def _():
            total[...] = jnp.zeros_like(total)

        gate = dot(source[...], joined(weights, gate_at), 1, 0)
        up = dot(source[...], joined(weights, up_at), 1, 0)
        hidden = gate * (1.0 / (1.0 + jnp.exp(-gate))) * up
        hidden = unit_mask(tile, units, hidden).astype(BF)
        gate_ref[...] = gate.astype(BF)
        up_ref[...] = up.astype(BF)
        hidden_ref[...] = hidden
        total[...] += dot(hidden, unit_mask(tile, units, joined(weights, down_at)), 1, 1)

        @pl.when(tile == steps - 1)
        def _():
            put_chunks(place, outs, total)

    by_tile = lambda rows: pl.BlockSpec((rows, UNIT_TILE), lambda f, place: (0, f))
    found = call(
        kernel,
        [shape((tokens, units))] * 3 + [shape((tokens // chunks, width)) for _ in range(chunks)],
        [second_in] + list(ffn),
        queue,
        grid=(steps,),
        in_specs=[None] + [by_tile(part.shape[0]) for part in ffn],
        out_specs=[by_tile(tokens)] * 3 + [None] * chunks,
        scratch=[pltpu.VMEM((tokens, width), F32)],
    )
    return found[:3], found[3:]


def feed_back(grad_low, gate, up, ffn, at_of, queue):
    tokens, width = grad_low.shape
    units = gate.shape[1]
    many = len(ffn)
    chunks = 1
    steps = pl.cdiv(units, UNIT_TILE)
    gate_at, up_at, down_at = at_of

    def kernel(place, source, gate_ref, up_ref, *refs):
        weights, refs = refs[:many], refs[many:]
        grad_gate_ref, grad_up_ref, outs, total = refs[0], refs[1], refs[2:-1], refs[-1]
        tile = pl.program_id(0)

        @pl.when(tile == 0)
        def _():
            total[...] = jnp.zeros_like(total)

        grad_hidden = dot(source[...], joined(weights, down_at), 1, 0)
        gate, up = gate_ref[...].astype(F32), up_ref[...].astype(F32)
        sigma = 1.0 / (1.0 + jnp.exp(-gate))
        grad_gate = grad_hidden * up * sigma * (1.0 + gate * (1.0 - sigma))
        grad_up = grad_hidden * gate * sigma
        grad_gate = unit_mask(tile, units, grad_gate).astype(BF)
        grad_up = unit_mask(tile, units, grad_up).astype(BF)
        grad_gate_ref[...] = grad_gate
        grad_up_ref[...] = grad_up
        both = jnp.concatenate([grad_gate, grad_up], axis=1)
        gate_w = unit_mask(tile, units, joined(weights, gate_at))
        up_w = unit_mask(tile, units, joined(weights, up_at))
        total[...] += dot(both, jnp.concatenate([gate_w, up_w], axis=1), 1, 1)

        @pl.when(tile == steps - 1)
        def _():
            put_chunks(place, outs, total)

    by_tile = lambda rows: pl.BlockSpec((rows, UNIT_TILE), lambda f, place: (0, f))
    found = call(
        kernel,
        [shape((tokens, units))] * 2 + [shape((tokens // chunks, width)) for _ in range(chunks)],
        [grad_low, gate, up] + list(ffn),
        queue,
        grid=(steps,),
        in_specs=[None, by_tile(tokens), by_tile(tokens)] + [by_tile(p.shape[0]) for p in ffn],
        out_specs=[by_tile(tokens)] * 2 + [None] * chunks,
        scratch=[pltpu.VMEM((tokens, width), F32)],
    )
    return found[:2], found[2:]


def summed_rows(source, rows):
    total = source[:rows, :].astype(F32)
    for at in range(rows, source.shape[0], rows):
        total += source[at : at + rows, :].astype(F32)
    return total


def add_and_norm(stream, chunks, gain, queue):
    def kernel(place, stream_ref, gain_ref, *refs):
        total, normed = refs[-2:]
        values = stream_ref[...].astype(F32)
        values += summed_rows(refs[0], values.shape[0])
        total[...] = values
        scale = lax.rsqrt(jnp.mean(values * values, axis=1, keepdims=True) + EPSILON)
        normed[...] = (values * scale * gain_ref[...]).astype(BF)

    outs = [shape(stream.shape, F32), shape(stream.shape)]
    return call(kernel, outs, [stream, gain] + list(chunks), queue)


def add_last(stream, chunks, queue):
    def kernel(place, stream_ref, *refs):
        values = stream_ref[...]
        values += summed_rows(refs[0], values.shape[0])
        refs[-1][...] = values.astype(BF)

    return call(kernel, [shape(stream.shape)], [stream] + list(chunks), queue)[0]


def norm_back(incoming, values, gain, chunks, queue):
    def kernel(place, incoming_ref, values_ref, gain_ref, *refs):
        total, low = refs[-2:]
        grad = summed_rows(refs[0], incoming_ref.shape[0])
        values = values_ref[...].astype(F32)
        scale = lax.rsqrt(jnp.mean(values * values, axis=1, keepdims=True) + EPSILON)
        unit = values * scale
        weighted = grad * gain_ref[...]
        inner = jnp.mean(weighted * unit, axis=1, keepdims=True)
        result = incoming_ref[...].astype(F32) + scale * (weighted - unit * inner)
        total[...] = result
        low[...] = result.astype(BF)

    outs = [shape(values.shape, F32), shape(values.shape)]
    ins = [incoming, values, gain] + list(chunks)
    return call(kernel, outs, ins, queue)


def weight_grads(groups, block, queue):
    width = groups[0][0][0].shape[1]
    sides = width // block // 2
    half = block // 2
    widths = [rights[0].shape[1] for _, rights in groups]
    wide = sum(widths)
    lefts, left_of = [], []
    for left, _ in groups:
        known = [k for k, other in enumerate(lefts) if other[0] is left[0]]
        left_of.append(known[0] if known else len(lefts))
        if not known:
            lefts.append(left)
    many = len(lefts[0])
    ins = [x for left in lefts for x in left] + [x for _, right in groups for x in right]
    read = len(ins)

    def terms(refs):
        joined_of = lambda k: jnp.concatenate([x[...] for x in refs[k * many : (k + 1) * many]], axis=0)
        left_all = [joined_of(k).T for k in range(len(lefts))]
        return [dot(left_all[at], joined_of(len(lefts) + k), 1, 0) for k, at in enumerate(left_of)]

    tokens = lefts[0][0].shape[0]
    cut = lambda first: pl.BlockSpec((tokens, block), lambda i, place: (0, first + i))
    in_specs = ([cut(0)] * (many // 2) + [cut(sides)] * (many // 2)) * len(lefts)
    in_specs += [None] * (len(groups) * many)

    if sides != 4:
        def kernel(place, *refs):
            at = 0
            for value, columns in zip(terms(refs[:read]), widths):
                refs[-1][:, at : at + columns] = value
                at += columns

        both = call(
            kernel,
            [shape((sides * block, wide), F32)],
            ins,
            queue,
            grid=(sides,),
            in_specs=in_specs,
            out_specs=[pl.BlockSpec((block, wide), lambda i, place: (i, 0))],
        )[0]
        yield None
        bit = sides // 2
        while bit:
            middle = both.shape[0] // 2
            both = both[:middle] + swap(both[middle:].astype(BF), "context", bit).astype(F32)
            bit //= 2
        none = jnp.zeros_like(both[:half])
        yield [both[:half], none, both[half:], none]
        return

    def weights(place, *refs):
        low_keep, low_send, high_keep, high_send = refs[read:]
        step = pl.program_id(0)
        found = terms(refs[:read])

        def write(target, start):
            at = 0
            for value, columns in zip(found, widths):
                target[:, at : at + columns] = value[start : start + half].astype(BF)
                at += columns

        for number, (low, high) in enumerate(
            ((low_keep, high_keep), (low_send, high_keep), (low_keep, high_send), (low_send, high_send))
        ):
            @pl.when(step == number)
            def _(low=low, high=high):
                write(low, 0)
                write(high, half)

    piece = lambda index: pl.BlockSpec((half, wide), index)
    low_keep, low_send, high_keep, high_send = call(
        weights,
        [shape((block, wide))] * 4,
        ins,
        queue,
        grid=(sides,),
        in_specs=in_specs,
        out_specs=[
            piece(lambda i, place: (i // 2, 0)),
            piece(lambda i, place: (i // 3, 0)),
            piece(lambda i, place: (jnp.minimum(i, 1), 0)),
            piece(lambda i, place: (i // 3, 0)),
        ],
    )
    low_got = swap(low_send, "context", 1)
    high_got = swap(high_send, "context", 2)
    yield None

    def fold(place, a, b, c, d, low_own, low_next, high_own, high_next):
        for first, second, own, next_ref in ((a, b, low_own, low_next), (c, d, high_own, high_next)):
            both = first[...].astype(F32) + second[...].astype(F32)
            own[...] = both[:half].astype(BF)
            next_ref[...] = both[half:].astype(BF)

    low_own, low_next, high_own, high_next = call(
        fold,
        [shape((half, wide))] * 4,
        [low_keep, low_got, high_keep, high_got],
        queue,
    )
    yield [low_own, swap(low_next, "context", 2), high_own, swap(high_next, "context", 1)]


def finish_ffn(parts, gate_w, up_w, queue):
    block, units = gate_w.shape
    half = block // 2

    def kernel(place, *refs):
        gate_ref, up_ref = refs[12:14]
        outs, sums = refs[14:17], refs[17]
        for k, out in enumerate(outs):
            a, b, c, d = refs[4 * k : 4 * k + 4]
            out[:half, :] = a[...].astype(F32) + b[...].astype(F32)
            out[half:, :] = c[...].astype(F32) + d[...].astype(F32)
        product = outs[0][...] * gate_ref[...].astype(F32) + outs[1][...] * up_ref[...].astype(F32)
        sums[...] = jnp.broadcast_to(jnp.sum(product, axis=1, keepdims=True), sums.shape)

    outs = [shape((block, units), F32)] * 3 + [shape((block, PAIR), F32)]
    return call(kernel, outs, [x for part in parts for x in part] + [gate_w, up_w], queue)


def finish_heads(parts, query_w, pair_w, queue):
    block, columns = query_w.shape
    half = parts[0].shape[0]

    def kernel(place, a, b, c, d, query_ref, pair_ref, query_out, output_out, pair_out, sums):
        for start, x, y in ((0, a, b), (half, c, d)):
            both = x[...].astype(F32) + y[...].astype(F32)
            rows = slice(start, start + half)
            query_out[rows, :] = both[:, :columns]
            output_out[rows, :] = both[:, columns : 2 * columns]
            pair_out[rows, :] = both[:, 2 * columns :]
        total = jnp.sum(query_out[...] * query_ref[...].astype(F32), axis=1, keepdims=True)
        total += jnp.sum(pair_out[...] * pair_ref[...].astype(F32), axis=1, keepdims=True)
        sums[...] = jnp.broadcast_to(total, sums.shape)

    outs = [shape((block, columns), F32)] * 2 + [shape((block, PAIR), F32)] * 2
    return call(kernel, outs, list(parts) + [query_w, pair_w], queue)


def per_device(hidden_input, cotangent, *params):
    layers = (params[:9], params[9:])
    tensor_count = lax.axis_size("tensor")
    context_count = lax.axis_size("context")
    sequences, _, rows, width = hidden_input.shape
    tokens = rows * tensor_count
    block = layers[0][1].shape[0]
    query_width = layers[0][1].shape[1]
    heads = query_width // HD
    heads_of = [j * heads // (H // KV) for j in range(tensor_count)]
    context = lax.axis_index("context")
    place = jnp.stack(
        [lax.axis_index("dp") * context_count + context, context, lax.axis_index("tensor")]
    ).astype(jnp.int32)
    streams = range(sequences)

    positions = context * tokens + jnp.arange(tokens, dtype=jnp.int32)
    freq = THETA ** (-2.0 * jnp.arange(HD // 2, dtype=F32) / HD)
    angle = positions.astype(F32)[:, None] * freq[None, :]
    cosine, sine = jnp.cos(angle), jnp.sin(angle)
    tables = (
        jnp.concatenate([cosine] * 4, axis=1),
        jnp.concatenate([-sine, sine] * 2, axis=1),
    )

    queue = Queue(place)

    me = lax.axis_index("tensor")
    gains = jnp.stack([layers[0][0], layers[0][5], layers[1][0], layers[1][5]], axis=1)
    gains = jnp.pad(gains, ((0, 0), (0, PAIR - 4)))
    wide_w = [w for layer in layers for w in (layer[2], layer[3])]
    small = []
    for k in range(tensor_count):
        head = ((me ^ k) * heads) // (H // KV)
        cut = [lax.dynamic_slice_in_dim(w, head * HD, HD, 1) for w in wide_w]
        piece = jnp.concatenate(cut + [gains], axis=1)
        small.append(swap(piece, "tensor", k) if k else piece)

    moved = reorder([hidden_input[i, 0] for i in streams] + [cotangent[i, 0] for i in streams], queue)
    first_low, incoming = moved[:sequences], moved[sequences:]
    normed = [[gather_tokens(low)] for low in first_low]
    grad_all = [gather_tokens(low) for low in incoming]

    stack_qo = lambda layer, due=(): gather_near(stacked([layer[1], layer[4]], place, due))
    stack_ffn = lambda layer, due=(): gather_near(stacked([layer[6], layer[7], layer[8]], place, due))
    qo_of, ffn_of = [stack_qo(layers[0]), None], [None, None]
    small = placed(small, queue)
    kvg = gather_near(small)
    qo_of[0] = gather_far(qo_of[0], queue)
    kvg = gather_far(kvg, queue)
    pairs_w = (small[:, :PAIR], small[:, PAIR : 2 * PAIR])
    gain_rows = small[:, 2 * PAIR :]
    kv_at = segments(kvg, 0, block, block)
    q_at = segments(qo_of[0], 0, block, block)
    o_at = segments(qo_of[0], block, 2 * block, block)
    gain_all = gain_vectors(kvg, kv_at, width, queue)
    gain_of = lambda number, part: gain_all[2 * number + part : 2 * number + part + 1]

    saved = [[{}, {}] for _ in streams]
    state = list(first_low)
    chunks = [None for _ in streams]

    def enter(number, i):
        keep = saved[i][number]
        keep["stream"] = state[i]
        gain = gain_of(0, 0) if number == 0 else None
        keep["query"], pair, keep["first_in"] = project(
            normed[i], gain, qo_of[number], q_at, (number, kvg), kv_at, tables, queue
        )
        keep["blocks"] = exchange_blocks([pair] * context_count)

    def mix(number, i):
        keep = saved[i][number]
        keep["mixed"], keep["stats"], out = attend(
            keep["query"], keep["blocks"], qo_of[number], o_at, number == 0, width, queue
        )
        chunks[i] = exchange_tokens(out)

    def between(number, i):
        keep = saved[i][number]
        keep["middle"], low = add_and_norm(state[i], chunks[i], gain_of(number, 1), queue)
        keep["second_in"] = gather_tokens(low)

    def forward_units(number, i):
        keep = saved[i][number]
        (keep["gate"], keep["up"], keep["hidden"]), out = feed(
            keep["second_in"], ffn_of[number], ffn_at, queue
        )
        chunks[i] = exchange_tokens(out)

    last = sequences - 1
    blocks_of = lambda number: [x for i in streams for x in saved[i][number]["blocks"]]
    for i in streams:
        enter(0, i)
    near = stack_ffn(layers[0], blocks_of(0))
    for i in streams:
        mix(0, i)
    ffn_of[0] = gather_far(near, queue, [saved[last][0]["stats"]])
    ffn_at = [segments(ffn_of[0], k * block, (k + 1) * block, block) for k in range(3)]
    qo_of[1] = gather_far(stack_qo(layers[1], ffn_of[0][1:5]), queue)
    ffn_of[1] = gather_far(stack_ffn(layers[1], qo_of[1][1:5]), queue)
    for i in streams:
        if i == last:
            queue.due = [grad_all[0]]
        between(0, i)
    for i in streams:
        if i == last:
            queue.due = list(qo_of[1])
        forward_units(0, i)
    for i in streams:
        if i == last:
            queue.due = list(ffn_of[1][1:3])
        state[i], low = add_and_norm(saved[i][0]["middle"], chunks[i], gain_of(1, 0), queue)
        normed[i] = [gather_tokens(low)]
    queue.due = list(ffn_of[1])
    for i in streams:
        enter(1, i)
    for i in streams:
        mix(1, i)
    for i in streams:
        between(1, i)
    for i in streams:
        forward_units(1, i)

    last_chunks = list(chunks)

    def add_out(i):
        state[i] = add_last(saved[i][1]["middle"], last_chunks[i], queue)

    def back_units(number, i):
        keep = saved[i][number]
        keep["grad_all"] = grad_all[i]
        (keep["grad_gate"], keep["grad_up"]), out = feed_back(
            grad_all[i], keep["gate"], keep["up"], ffn_of[number], ffn_at, queue
        )
        chunks[i] = exchange_tokens(out)

    def back_between(number, i):
        keep = saved[i][number]
        keep["grad_mid"], low = norm_back(
            incoming[i], keep["middle"], gain_of(number, 1), chunks[i], queue
        )
        keep["mid_all"] = gather_tokens(low)

    pieces = [None for _ in streams]

    def back_mix(number, i):
        keep = saved[i][number]
        keep["grad_query"], pieces[i] = attend_back(
            keep["mid_all"], keep["query"], keep["blocks"], keep["stats"], qo_of[number], o_at,
            tables, number == 0, queue,
        )
        pieces[i] = exchange_blocks(pieces[i])

    def back_enter(number, i):
        keep = saved[i][number]
        keep["grad_pair"], out = project_back(
            keep["grad_query"], pieces[i], qo_of[number], q_at, (number, kvg), kv_at, tables,
            width, queue,
        )
        chunks[i] = exchange_tokens(out)

    def leave(number, i):
        keep = saved[i][number]
        incoming[i], low = norm_back(
            keep["grad_mid"], keep["stream"], gain_of(number, 0), chunks[i], queue
        )
        if number == 1:
            grad_all[i] = gather_tokens(low)

    works, parts = [{}, {}], [{}, {}]
    crossed = {}

    def pair_of(number, name):
        own = [saved[i][number][name] for i in streams]
        if (number, name) not in crossed:
            crossed[number, name] = [swap(x, "dp", 1) for x in own]
        return own + crossed[number, name]

    def grads(number, key, *names):
        cache = {}
        for name in set(sum(names, ())):
            cache[name] = pair_of(number, name)
        works[number][key] = weight_grads(
            [(cache[left], cache[right]) for left, right in names], block, queue
        )
        next(works[number][key])

    def fold(number, key):
        parts[number][key] = next(works[number][key])

    def end(number, key):
        layer = layers[number]
        if key == "ffn":
            three = [parts[number][name] for name in ("gate", "up", "down")]
            summed[number][0] = finish_ffn(three, layer[6], layer[7], queue)
        else:
            summed[number][1] = finish_heads(parts[number][key], layer[1], pairs_w[number], queue)

    GATE = ("gate", ("second_in", "grad_gate"))
    UP = ("up", ("second_in", "grad_up"))
    DOWN = ("down", ("grad_all", "hidden"))
    HEADS = ("heads", ("first_in", "grad_query"), ("mid_all", "mixed"), ("first_in", "grad_pair"))
    summed = [[None, None], [None, None]]
    for number in (1, 0):
        for i in streams:
            back_units(number, i)
            if number == 1 and i == 0:
                add_out(0)
        if number == 0:
            fold(1, "down")
            fold(1, "heads")
        for i in streams:
            back_between(number, i)
        if number == 0:
            end(1, "ffn")
            end(1, "heads")
        grads(number, *GATE)
        grads(number, *UP)
        for i in streams:
            back_mix(number, i)
        fold(number, "gate")
        if number == 1:
            fold(1, "up")
            for i in streams[1:]:
                add_out(i)
        back_enter(number, 0)
        if number == 0:
            fold(0, "up")
        for i in streams[1:]:
            back_enter(number, i)
        grads(number, *DOWN)
        leave(number, 0)
        if number == 0:
            grads(0, *HEADS)
            fold(0, "down")
        for i in streams[1:]:
            leave(number, i)
        if number == 1:
            grads(1, *HEADS)
        else:
            end(0, "ffn")
            fold(0, "heads")
    outputs = jnp.stack(reorder(state, queue))
    in_grads = jnp.stack(reorder(incoming, queue))
    end(0, "heads")

    sums = []
    for number in range(2):
        own_gains = gain_rows[:, 2 * number : 2 * number + 2].astype(F32)
        sums.append(summed[number][1][3][:, :1] / own_gains[:, :1])
        sums.append(summed[number][0][3][:, :1] / own_gains[:, 1:])
    tail = jnp.pad(jnp.concatenate(sums, axis=1), ((0, 0), (0, PAIR - 4)))
    small_g = lax.all_to_all(
        jnp.concatenate([summed[0][1][2], summed[1][1][2], tail], axis=1),
        "tensor", split_axis=0, concat_axis=0, tiled=True,
    ).reshape(tensor_count, -1, 3 * PAIR)
    gain_g = jnp.sum(small_g[:, :, 2 * PAIR : 2 * PAIR + 4], axis=0)

    results = [
        outputs.reshape(hidden_input.shape),
        in_grads.reshape(hidden_input.shape),
    ]
    for number in range(2):
        ffn_g, head_g = summed[number]
        pair_g = []
        for part in range(2):
            at = (2 * number + part) * HD
            by_head = []
            for head in range(KV):
                pieces = [
                    small_g[j, :, at : at + HD] for j in range(tensor_count) if heads_of[j] == head
                ]
                by_head.append(sum(pieces))
            pair_g.append(jnp.concatenate(by_head, axis=1))
        results += [
            gain_g[:, 2 * number],
            head_g[0],
            pair_g[0],
            pair_g[1],
            head_g[1],
            gain_g[:, 2 * number + 1],
            ffn_g[0],
            ffn_g[1],
            ffn_g[2],
        ]
    return tuple(results)


def solution(mesh):
    rows = P(("dp", "context", "tensor"))
    tall = P(("dp", "context", "tensor"), None)
    wide = P(("dp", "context"), "tensor")
    tokens = P(None, "dp", ("context", "tensor"), None)
    layer = (rows, wide, tall, tall, wide, rows, wide, wide, wide)
    return jax.shard_map(
        per_device,
        mesh=mesh,
        in_specs=(tokens, tokens) + layer + layer,
        out_specs=(tokens, tokens) + layer + layer,
        check_vma=False,
    )
```
